32 devices in a mesh: ctx: 16 (over z, y, core), fsdp: 2 (over x).
Axes of the slice: x: 2, y: 2, z: 4, core: 2. Of those that a mesh axis runs over, the one named last changes fastest.
Arguments:
- tokens: bfloat16 [24, 1024, 896], P('fsdp', 'ctx'), may hold values from -6 to 6
- positions: int32 [24, 1024], P('fsdp', 'ctx'), may hold values from 0 to 1023, as said below
- cotangent: bfloat16 [24, 1024, 896], P('fsdp', 'ctx'), may hold values from -6 to 6
- query_weight: bfloat16 [896, 896], P('fsdp'), may hold values from -0.1875 to 0.1875
- key_weight: bfloat16 [896, 128], P('fsdp'), may hold values from -0.1875 to 0.1875
- value_weight: bfloat16 [896, 128], P('fsdp'), may hold values from -0.1875 to 0.1875
- out_weight: bfloat16 [896, 896], P('fsdp'), may hold values from -0.75 to 0.75
- gate_weight: bfloat16 [896, 4864], P('fsdp'), may hold values from -0.1875 to 0.1875
- up_weight: bfloat16 [896, 4864], P('fsdp'), may hold values from -0.1875 to 0.1875
- down_weight: bfloat16 [4864, 896], P('fsdp'), may hold values from -0.078125 to 0.078125
- query_bias: bfloat16 [896], P('fsdp'), may hold values from -3 to 3
- key_bias: bfloat16 [128], P('fsdp'), may hold values from -3 to 3
- value_bias: bfloat16 [128], P('fsdp'), may hold values from -3 to 3
- first_gain: bfloat16 [896], P('fsdp'), may hold values from 0.099609375 to 1.8984375
- second_gain: bfloat16 [896], P('fsdp'), may hold values from 0.099609375 to 1.8984375
Outputs:
- mixed: bfloat16 [24, 1024, 896], P('fsdp', 'ctx')
- grad_tokens: float32 [24, 1024, 896], P('fsdp', 'ctx')
- grad_query_weight: float32 [896, 896], P('fsdp')
- grad_key_weight: float32 [896, 128], P('fsdp')
- grad_value_weight: float32 [896, 128], P('fsdp')
- grad_out_weight: float32 [896, 896], P('fsdp')
- grad_gate_weight: float32 [896, 4864], P('fsdp')
- grad_up_weight: float32 [896, 4864], P('fsdp')
- grad_down_weight: float32 [4864, 896], P('fsdp')
- grad_query_bias: float32 [896], P('fsdp')
- grad_key_bias: float32 [128], P('fsdp')
- grad_value_bias: float32 [128], P('fsdp')
- grad_first_gain: float32 [896], P('fsdp')
- grad_second_gain: float32 [896], P('fsdp')
The draws below stay inside these ranges and needn't reach their ends.
Inputs may be any that keep to these rules, and one draw needn't show every extreme that they name: Each sequence's row is an ordering of 0 to 1023 built from blocks of 32 consecutive positions in rising order; each run of 64 stored entries that one index of ctx holds is block p followed by block 31 - p, with p differing from run to run.
All inputs are finite; a program needn't handle non-finite values.
Results may differ from the reference program's by a relative error of at most 0.02.
Values may be sent and summed in bfloat16 or wider, within the bound.
No kernel may reach another device: no remote copies, remote signals or barrier semaphores. Data moves between devices by JAX's collectives and lax.ppermute only.
A program may use at most 256 MiB of HBM per device.

```python
import math
import jax
import jax.numpy as jnp
from jax import lax

D = 896
Q_HEADS = 14
KV_HEADS = 2
HEAD_DIM = 64
FF = 4864
BLK = 32
SEQ_LEN = 1024
SEQS = 24
KV_WIDTH = 128


def draw_positions(key, part):
    key = jax.random.fold_in(key, 1)
    pairs = SEQ_LEN // (2 * BLK)
    keys = jax.random.split(key, SEQS)
    orders = jax.vmap(lambda single: jax.random.permutation(single, pairs))(keys).astype(jnp.int32)
    offsets = jnp.arange(BLK, dtype=jnp.int32)
    front = orders[:, :, None] * BLK + offsets
    back = (2 * pairs - 1 - orders)[:, :, None] * BLK + offsets
    return jnp.concatenate([front, back], axis=2).reshape(SEQS, SEQ_LEN).astype(jnp.int32)


def level_of(own_key, dims, pieces, low, top_value):
    factor_of = 1.0
    for position, blocks in pieces:
        draws = jax.random.uniform(jax.random.fold_in(jax.random.fold_in(own_key, 6), position), (blocks,), jnp.float32, low / len(pieces), top_value / len(pieces))
        factor_of = factor_of * jnp.repeat(jnp.exp(draws), dims[position] // blocks).reshape((-1,) + (1,) * (len(dims) - 1 - position))
    return factor_of


def noise(key, extent, spread, limit, cuts=(), held_as=jnp.bfloat16):
    array = spread * jax.random.normal(key, extent, jnp.float32)
    if cuts:
        array = array * level_of(key, extent, cuts, -0.22, 0.18)
    return jnp.clip(array, -limit, limit).astype(held_as)


def setup_inputs(seed: int = 0) -> dict:
    key_list = jax.random.split(jax.random.key(seed), 16)
    return {
        "tokens": noise(key_list[0], (SEQS, SEQ_LEN, D), 1.0, 6.0, ((0, 2), (1, 16))),
        "positions": draw_positions(jax.random.fold_in(key_list[15], 71), 0),
        "cotangent": noise(key_list[2], (SEQS, SEQ_LEN, D), 1.0, 6.0, ((0, 2), (1, 16))),
        "query_weight": noise(key_list[3], (D, D), D ** -0.5, 0.1875, ((0, 2),)),
        "key_weight": noise(key_list[4], (D, KV_WIDTH), D ** -0.5, 0.1875, ((0, 2),)),
        "value_weight": noise(key_list[5], (D, KV_WIDTH), D ** -0.5, 0.1875, ((0, 2),)),
        "out_weight": noise(key_list[6], (D, D), (D // 16) ** -0.5, 0.75, ((0, 2),)),
        "gate_weight": noise(key_list[7], (D, FF), D ** -0.5, 0.1875, ((0, 2),)),
        "up_weight": noise(key_list[8], (D, FF), D ** -0.5, 0.1875, ((0, 2),)),
        "down_weight": noise(key_list[9], (FF, D), FF ** -0.5, 0.078125, ((0, 2),)),
        "query_bias": noise(key_list[10], (D,), 0.5, 3.0, ((0, 2),)),
        "key_bias": noise(key_list[11], (KV_WIDTH,), 0.5, 3.0, ((0, 2),)),
        "value_bias": noise(key_list[12], (KV_WIDTH,), 0.5, 3.0, ((0, 2),)),
        "first_gain": jnp.clip(1.0 + 0.18 * jax.random.normal(key_list[13], (D,), jnp.float32), 0.099609375, 1.8984375).astype(jnp.bfloat16),
        "second_gain": jnp.clip(1.0 + 0.18 * jax.random.normal(key_list[14], (D,), jnp.float32), 0.099609375, 1.8984375).astype(jnp.bfloat16),
    }


epsilon = 1e-06
theta = 1000000.0

@jax.custom_vjp
def low(v):
    return lax.optimization_barrier(v.astype(jnp.bfloat16)).astype(jnp.float32)

@jax.custom_vjp
def low_back(v):
    return v

def low_keep(v):
    return (low(v), None)

def low_pass(kept, grad):
    return (grad,)

def back_keep(v):
    return (v, None)

def back_low(kept, grad):
    return (low(grad),)
low.defvjp(low_keep, low_pass)
low_back.defvjp(back_keep, back_low)

def rms_scale(rows, gain):
    inverse = lax.rsqrt(lax.optimization_barrier(jnp.mean(rows * rows, axis=-1, keepdims=True)) + epsilon)
    return rows * inverse * gain

def rope_tables(places, half):
    freq = theta ** (-jnp.arange(half, dtype=jnp.float32) / half)
    angles = places.astype(jnp.float32)[..., None] * freq
    return (jnp.cos(angles), jnp.sin(angles))

def rotate(values, cosine, sine):
    half = values.shape[-1] // 2
    front = values[..., :half]
    back = values[..., half:]
    cos_b = cosine[..., None, :]
    sin_b = sine[..., None, :]
    return jnp.concatenate([front * cos_b - back * sin_b, back * cos_b + front * sin_b], axis=-1)

def project(left, right):
    return jnp.dot(left, right, precision=lax.Precision.HIGHEST)

def layer(inputs, places, weights):
    query_weight, key_weight, value_weight, out_weight, gate_weight, up_weight, down_weight, query_bias, key_bias, value_bias, first_gain, second_gain = weights
    length = inputs.shape[0]
    group = Q_HEADS // KV_HEADS
    scale = 1.0 / math.sqrt(HEAD_DIM)
    first = low(rms_scale(inputs, first_gain))
    query_pre = low_back(project(first, query_weight) + query_bias)
    key_pre = low_back(project(first, key_weight) + key_bias)
    value = low(low_back(project(first, value_weight) + value_bias))
    cosine, sine = rope_tables(places, HEAD_DIM // 2)
    query_rot = low(rotate(query_pre.reshape(length, Q_HEADS, HEAD_DIM), cosine, sine))
    key_rot = low(rotate(key_pre.reshape(length, KV_HEADS, HEAD_DIM), cosine, sine))
    allowed = places[None, :] <= places[:, None]

    def one_group(items):
        query_part, key_part, value_part = items
        raw = low_back(jnp.einsum('qjd,kd->jqk', query_part, key_part, precision=lax.Precision.HIGHEST))
        masked = jnp.where(allowed[None], raw * scale, -1000000000.0)
        top = lax.optimization_barrier(jnp.max(masked, axis=-1, keepdims=True))
        expo = jnp.exp(masked - top)
        probs = expo / lax.optimization_barrier(jnp.sum(expo, axis=-1, keepdims=True))
        return jnp.einsum('jqk,kd->qjd', low(probs), value_part, precision=lax.Precision.HIGHEST)
    query_groups = jnp.moveaxis(query_rot.reshape(length, KV_HEADS, group, HEAD_DIM), 1, 0)
    key_groups = jnp.moveaxis(key_rot, 1, 0)
    value_groups = jnp.moveaxis(value.reshape(length, KV_HEADS, HEAD_DIM), 1, 0)
    outputs = lax.map(jax.checkpoint(one_group), (query_groups, key_groups, value_groups))
    attn = low(low_back(jnp.moveaxis(outputs, 0, 1).reshape(length, Q_HEADS * HEAD_DIM)))
    middle = inputs + low_back(project(attn, out_weight))
    second = low(rms_scale(middle, second_gain))
    gate = low_back(project(second, gate_weight))
    up_part = low_back(project(second, up_weight))
    hidden = low(jax.nn.silu(gate) * up_part)
    return middle + low_back(project(hidden, down_weight))

def reference(tokens, positions, cotangent, query_weight, key_weight, value_weight, out_weight, gate_weight, up_weight, down_weight, query_bias, key_bias, value_bias, first_gain, second_gain):
    weights = tuple((w.astype(jnp.float32) for w in (query_weight, key_weight, value_weight, out_weight, gate_weight, up_weight, down_weight, query_bias, key_bias, value_bias, first_gain, second_gain)))

    def per_sequence(totals, items):
        seq_tokens, seq_places, seq_grad = items
        inputs = seq_tokens.astype(jnp.float32)
        result, pull = jax.vjp(lambda rows, params: layer(rows, seq_places, params), inputs, weights)
        grad_rows, grad_params = pull(seq_grad.astype(jnp.float32))
        totals = tuple((a + b for a, b in zip(totals, grad_params)))
        return (totals, (result.astype(jnp.bfloat16), grad_rows))
    zeros = tuple((jnp.zeros_like(w) for w in weights))
    totals, outputs = lax.scan(per_sequence, zeros, (tokens, positions, cotangent))
    mixed, grad_tokens = outputs
    return (mixed, grad_tokens, totals[0], totals[1], totals[2], totals[3], totals[4], totals[5], totals[6], totals[7], totals[8], totals[9], totals[10], totals[11])
```

```python
import functools

import jax
import jax.numpy as jnp
from jax import lax
from jax.experimental import pallas as pl
from jax.experimental.pallas import tpu as pltpu
from jax.sharding import Mesh, PartitionSpec as P

Q_HEADS = 14
KV_HEADS = 2
HEAD_DIM = 64
GROUP = Q_HEADS // KV_HEADS
HALF = HEAD_DIM // 2
BLK = 32
CORES = 2
Q_WIDTH = GROUP * HEAD_DIM

epsilon = 1e-06
theta = 1000000.0
scale = HEAD_DIM ** (-0.5)

BF = jnp.bfloat16
F32 = jnp.float32
CHIPS = ("cz", "cy")
VMEM = 56 * 1024 * 1024
SWAP = [(0, 1), (1, 0)]
NT = (((1,), (1,)), ((), ()))
TN = (((0,), (0,)), ((), ()))


def swap(values, axis):
    return lax.ppermute(values, axis, SWAP)


def dot(left, right, dims=(((1,), (0,)), ((), ()))):
    return lax.dot_general(left, right, dims, preferred_element_type=F32)


def rms_scale(rows, gain):
    inverse = lax.rsqrt(jnp.mean(rows * rows, axis=-1, keepdims=True) + epsilon)
    return rows * inverse * gain


def project_kernel(x_ref, gain_ref, w_ref, b_ref, cos_ref, sin_ref, first_ref, q_ref, kv_ref):
    rows = x_ref[...].astype(F32)
    first = rms_scale(rows, gain_ref[...]).astype(BF)
    first_ref[...] = first
    pre = dot(first, w_ref[...]) + b_ref[...]
    turned = Q_WIDTH + HEAD_DIM
    cosine = jnp.concatenate([cos_ref[...]] * (turned // 128), axis=1)
    sine = jnp.concatenate([sin_ref[...]] * (turned // 128), axis=1)
    front = pre[:, :turned]
    lane = lax.broadcasted_iota(jnp.int32, front.shape, 1) % HEAD_DIM
    other = jnp.where(
        lane < HALF, pltpu.roll(front, turned - HALF, 1), pltpu.roll(front, HALF, 1)
    )
    rot = front * cosine + other * sine
    q_ref[...] = (rot[:, :Q_WIDTH] * scale).astype(BF)
    kv_ref[...] = jnp.concatenate([rot[:, Q_WIDTH:], pre[:, turned:]], axis=1).astype(BF)


def project(rows, gain, weight, bias, cosine, sine):
    count, width = rows.shape
    wide = weight.shape[1]
    step = 256
    row_block = lambda n: pl.BlockSpec((step, n), lambda i: (i, 0))
    whole = lambda a, b: pl.BlockSpec((a, b), lambda i: (0, 0))
    return pl.pallas_call(
        project_kernel,
        grid=(count // step,),
        in_specs=[
            row_block(width),
            whole(1, width),
            whole(width, wide),
            whole(1, wide),
            row_block(128),
            row_block(128),
        ],
        out_specs=[row_block(width), row_block(Q_WIDTH), row_block(2 * HEAD_DIM)],
        out_shape=[
            jax.ShapeDtypeStruct((count, width), BF),
            jax.ShapeDtypeStruct((count, Q_WIDTH), BF),
            jax.ShapeDtypeStruct((count, 2 * HEAD_DIM), BF),
        ],
        compiler_params=pltpu.CompilerParams(vmem_limit_bytes=VMEM),
        cost_estimate=pl.CostEstimate(
            flops=2 * count * width * wide, bytes_accessed=count * width * 4, transcendentals=0
        ),
    )(rows, gain, weight, bias, cosine, sine)


def stack_heads(flat):
    return jnp.concatenate(
        [flat[:, h * HEAD_DIM : (h + 1) * HEAD_DIM] for h in range(GROUP)], axis=0
    )


def fill_bias(offset, starts_ref, qpos_ref, bias_ref):
    own = qpos_ref[0]
    inside = lax.broadcasted_iota(jnp.int32, (BLK, own.shape[1]), 0)
    seq = pl.program_id(0) + offset
    for j in range(bias_ref.shape[0] // BLK):
        far = inside + starts_ref[seq, j]
        bias_ref[j * BLK : (j + 1) * BLK, :] = jnp.where(far <= own, 0.0, -1e30)


def query_chunks(local):
    total = GROUP * local
    return [(lo, min(lo + 2 * local, total)) for lo in range(0, total, 2 * local)]


def attend_kernel(offset, starts_ref, qpos_ref, q_ref, kv_ref, o_ref, lse_ref, bias_ref):
    local = 2 * q_ref.shape[2]
    keys = bias_ref.shape[0]
    fill_bias(offset, starts_ref, qpos_ref, bias_ref)
    kv = kv_ref[...].reshape(keys, 2 * HEAD_DIM)
    key = kv[:, :HEAD_DIM]
    value_t = kv.astype(F32).T[HEAD_DIM:].astype(BF)
    query = stack_heads(q_ref[...].reshape(local, Q_WIDTH))
    heads = []
    for lo, hi in query_chunks(local):
        bias = jnp.concatenate([bias_ref[...]] * ((hi - lo) // local), axis=1)
        scores = dot(key, query[lo:hi], NT) + bias
        top = jnp.max(scores, axis=0, keepdims=True)
        expo = jnp.exp(scores - top)
        total = jnp.sum(expo, axis=0, keepdims=True)
        out = dot(value_t, expo.astype(BF)) / total
        lse_ref[0, :, lo:hi] = top + jnp.log(total)
        heads += [out[:, at : at + local].T for at in range(0, hi - lo, local)]
    o_ref[...] = jnp.concatenate(heads, axis=1).astype(BF).reshape(o_ref.shape)


def attend_back_kernel(
    offset,
    starts_ref,
    qpos_ref,
    q_ref,
    kv_ref,
    do_ref,
    lse_ref,
    cos_ref,
    sin_ref,
    dq_ref,
    dkv_ref,
    bias_ref,
    probs_ref,
    grads_ref,
):
    local = 2 * q_ref.shape[2]
    keys = bias_ref.shape[0]
    fill_bias(offset, starts_ref, qpos_ref, bias_ref)
    kv = kv_ref[...].reshape(keys, 2 * HEAD_DIM)
    key = kv[:, :HEAD_DIM]
    value = kv[:, HEAD_DIM:]
    key_t = kv.astype(F32).T[:HEAD_DIM].astype(BF)
    query = stack_heads(q_ref[...].reshape(local, Q_WIDTH))
    grad_o = stack_heads(do_ref[...].reshape(local, Q_WIDTH))
    cosine = cos_ref[0]
    sine = sin_ref[0]
    heads = []
    for lo, hi in query_chunks(local):
        bias = jnp.concatenate([bias_ref[...]] * ((hi - lo) // local), axis=1)
        scores = dot(key, query[lo:hi], NT) + bias
        probs = jnp.exp(scores - lse_ref[0, :, lo:hi])
        probs_ref[:, lo:hi] = probs.astype(BF)
        grad_p = dot(value, grad_o[lo:hi], NT)
        inner = jnp.sum(probs * grad_p, axis=0, keepdims=True)
        grad_s = (probs * (grad_p - inner)).astype(BF)
        grads_ref[:, lo:hi] = grad_s
        grad_q = dot(key_t, grad_s) * scale
        for at in range(0, hi - lo, local):
            front = grad_q[:HALF, at : at + local]
            back = grad_q[HALF:, at : at + local]
            turned = jnp.concatenate(
                [front * cosine + back * sine, back * cosine - front * sine], axis=0
            )
            heads.append(turned.T)
    dq_ref[...] = jnp.concatenate(heads, axis=1).astype(BF).reshape(dq_ref.shape)
    grad_k = dot(grads_ref[...], query)
    grad_v = dot(probs_ref[...], grad_o)
    dkv_ref[...] = jnp.concatenate([grad_k, grad_v], axis=1).astype(BF).reshape(dkv_ref.shape)


def attention(back, offset, seqs, starts, qpos, q, kv, *more):
    run = q.shape[2]
    chips = kv.shape[0]
    local = 2 * run
    keys = chips * local
    total = GROUP * local
    q_spec = pl.BlockSpec((2, 1, run, Q_WIDTH), lambda s, st: (0, s + offset, 0, 0))
    part_spec = pl.BlockSpec((2, 1, run, Q_WIDTH), lambda s, st: (0, s, 0, 0))
    kv_block = (chips, 2, 1, run, 2 * HEAD_DIM)
    kv_spec = pl.BlockSpec(kv_block, lambda s, st: (0, 0, s + offset, 0, 0))
    kv_part_spec = pl.BlockSpec(kv_block, lambda s, st: (0, 0, s, 0, 0))
    lse_spec = pl.BlockSpec((1, 1, total), lambda s, st: (s + offset, 0, 0))
    qpos_spec = pl.BlockSpec((1, 1, local), lambda s, st: (s + offset, 0, 0))
    turn_spec = pl.BlockSpec((1, HALF, local), lambda s, st: (s + offset, 0, 0))
    in_specs = [qpos_spec, q_spec, kv_spec]
    scratch = [pltpu.VMEM((keys, local), F32)]
    part_shape = jax.ShapeDtypeStruct((2, seqs, run, Q_WIDTH), BF)
    if back:
        in_specs += [q_spec, lse_spec, turn_spec, turn_spec]
        out_specs = [part_spec, kv_part_spec]
        kv_shape = kv.shape[:2] + (seqs,) + kv.shape[3:]
        out_shape = [part_shape, jax.ShapeDtypeStruct(kv_shape, BF)]
        scratch += [pltpu.VMEM((keys, total), BF)] * 2
    else:
        out_specs = [part_spec, lse_spec]
        out_shape = [part_shape, jax.ShapeDtypeStruct((seqs, 1, total), F32)]
    passes = 5 if back else 2
    return pl.pallas_call(
        functools.partial(attend_back_kernel if back else attend_kernel, offset),
        grid_spec=pltpu.PrefetchScalarGridSpec(
            num_scalar_prefetch=1,
            grid=(seqs,),
            in_specs=in_specs,
            out_specs=out_specs,
            scratch_shapes=scratch,
        ),
        out_shape=out_shape,
        compiler_params=pltpu.CompilerParams(vmem_limit_bytes=VMEM),
        cost_estimate=pl.CostEstimate(
            flops=8 * passes * seqs * keys * total * HEAD_DIM,
            bytes_accessed=seqs * keys * 512,
            transcendentals=seqs * keys * total,
        ),
    )(starts, qpos, q, kv, *more)


def mlp_kernel(s_ref, c_ref, g_ref, u_ref, d_ref, hid_ref, gg_ref, gu_ref, mix_ref, gs_ref):
    rows = s_ref[...]
    grad = c_ref[...]
    wide = g_ref.shape[1]
    for lo in range(0, wide, 256):
        hi = min(lo + 256, wide)
        gate = dot(rows, g_ref[:, lo:hi])
        up = dot(rows, u_ref[:, lo:hi])
        grad_hidden = dot(grad, d_ref[lo:hi, :], NT)
        sig = 1.0 / (1.0 + jnp.exp(-gate))
        silu = gate * sig
        hid_ref[:, lo:hi] = (silu * up).astype(BF)
        gg_ref[:, lo:hi] = (grad_hidden * up * (sig * (1.0 + gate * (1.0 - sig)))).astype(BF)
        gu_ref[:, lo:hi] = (grad_hidden * silu).astype(BF)
    mix_ref[...] = dot(hid_ref[...], d_ref[...]).astype(BF)
    gs_ref[...] = (dot(gg_ref[...], g_ref[...], NT) + dot(gu_ref[...], u_ref[...], NT)).astype(BF)


def mlp(rows, grad, gate_w, up_w, down_w):
    count, width = rows.shape
    wide = gate_w.shape[1]
    step = 256
    row_block = lambda n: pl.BlockSpec((step, n), lambda i: (i, 0))
    whole = lambda a, b: pl.BlockSpec((a, b), lambda i: (0, 0))
    shape = lambda n: jax.ShapeDtypeStruct((count, n), BF)
    return pl.pallas_call(
        mlp_kernel,
        grid=(count // step,),
        in_specs=[
            row_block(width),
            row_block(width),
            whole(width, wide),
            whole(width, wide),
            whole(wide, width),
        ],
        out_specs=[row_block(wide)] * 3 + [row_block(width)] * 2,
        out_shape=[shape(wide)] * 3 + [shape(width)] * 2,
        compiler_params=pltpu.CompilerParams(vmem_limit_bytes=VMEM),
        cost_estimate=pl.CostEstimate(
            flops=12 * count * width * wide,
            bytes_accessed=count * (wide * 6 + width * 8),
            transcendentals=count * wide,
        ),
    )(rows, grad, gate_w, up_w, down_w)


def weight_grad_kernel(a_near, a_far, b_near, b_far, out_ref, acc_ref):
    step = pl.program_id(0)
    steps = pl.num_programs(0)

    @pl.when(step == 0)
    def _():
        acc_ref[...] = dot(a_near[...], b_near[...], TN)

    @pl.when(jnp.logical_and(step > 0, step < steps // 2))
    def _():
        acc_ref[...] += dot(a_near[...], b_near[...], TN)

    @pl.when(jnp.logical_and(step >= steps // 2, step < steps - 1))
    def _():
        acc_ref[...] += dot(a_far[...], b_far[...], TN)

    @pl.when(step == steps - 1)
    def _():
        out_ref[...] = (acc_ref[...] + dot(a_far[...], b_far[...], TN)).astype(BF)


def weight_grad(near, far):
    (a_near, b_near), (a_far, b_far) = near, far
    count, high = a_near.shape
    wide = b_near.shape[1]
    half = 2
    step = count // half
    near_block = lambda n: pl.BlockSpec((step, n), lambda i: (jnp.minimum(i, half - 1), 0))
    far_block = lambda n: pl.BlockSpec((step, n), lambda i: (jnp.maximum(i - half, 0), 0))
    return pl.pallas_call(
        weight_grad_kernel,
        grid=(2 * half,),
        in_specs=[near_block(high), far_block(high), near_block(wide), far_block(wide)],
        out_specs=pl.BlockSpec((high, wide), lambda i: (0, 0)),
        out_shape=jax.ShapeDtypeStruct((high, wide), BF),
        scratch_shapes=[pltpu.VMEM((high, wide), F32)],
        compiler_params=pltpu.CompilerParams(vmem_limit_bytes=VMEM),
        cost_estimate=pl.CostEstimate(
            flops=4 * count * high * wide,
            bytes_accessed=4 * count * (high + wide),
            transcendentals=0,
        ),
    )(a_near, a_far, b_near, b_far)


def gather_small(values, axis, size):
    out = values[None]
    index = lax.axis_index(axis)
    bit = 1
    while bit < size:
        other = lax.ppermute(out, axis, [(i, i ^ bit) for i in range(size)])
        low = (index & bit) == 0
        out = jnp.where(
            low, jnp.concatenate([out, other], axis=0), jnp.concatenate([other, out], axis=0)
        )
        bit *= 2
    return out


def line_part(values, at):
    at = jnp.clip(at, 0, values.shape[0] - 1)
    return lax.dynamic_index_in_dim(values, at, 0, keepdims=False).astype(F32)


def line_load(values, axis, step, arrived):
    size = values.shape[0]
    index = lax.axis_index(axis)
    far = size - 1 - step
    up, down = line_part(values, index + far), line_part(values, index - far)
    if step:
        up, down = up + arrived[0].astype(F32), down + arrived[1].astype(F32)
    return up.astype(BF), down.astype(BF)


def line_send(load, axis, size, step):
    far = size - 1 - step
    right = [(i, i + 1) for i in range(size - 1) if i <= step]
    left = [(i + 1, i) for i in range(size - 1) if i + 1 >= far]
    return lax.ppermute(load[0], axis, right), lax.ppermute(load[1], axis, left)


def line_total(values, axis, arrived):
    own = line_part(values, lax.axis_index(axis))
    return (own + arrived[0].astype(F32) + arrived[1].astype(F32)).astype(BF)


def line_gather(values, axis, size):
    index = lax.axis_index(axis)
    right = left = values
    rights, lefts = [], []
    for step in range(size - 1):
        right = lax.ppermute(right, axis, [(i, i + 1) for i in range(size - 1) if i >= step])
        left = lax.ppermute(
            left, axis, [(i + 1, i) for i in range(size - 1) if i + 1 <= size - 1 - step]
        )
        rights.append(right)
        lefts.append(left)
    row = jnp.stack(rights[::-1] + [values] + lefts)
    return lax.dynamic_slice_in_dim(row, size - 1 - index, size, 0)


def pair_sum(values, axis, size):
    bit = 1
    while bit < size:
        other = lax.ppermute(values, axis, [(i, i ^ bit) for i in range(size)])
        values = (values.astype(F32) + other.astype(F32)).astype(values.dtype)
        bit *= 2
    return values


def after(first, *rest):
    return lax.optimization_barrier((first, *rest))[1:]


def make_body(sizes):
    cz, outer = sizes["cz"], sizes["outer"]
    chips = cz * sizes["cy"]
    owners = 2 * outer

    def ordered(axis, own, other):
        low = lax.axis_index(axis) == 0
        return jnp.where(low, own, other), jnp.where(low, other, own)

    def gather_rows(values):
        rows = values.shape[0]
        if outer > 1:
            values = lax.all_gather(values, "outer", axis=0)
        else:
            values = values[None]
        both = jnp.stack(ordered("pair", values, swap(values, "pair")), axis=1)
        return both.reshape((owners * rows,) + values.shape[2:])

    def sum_owners(values):
        split = values.reshape(outer, 2, -1, values.shape[1])
        if outer > 1:
            split = lax.psum_scatter(split, "outer", scatter_dimension=0)
        else:
            split = split[0]
        low = lax.axis_index("pair") == 0
        keep = jnp.where(low, split[0], split[1])
        send = jnp.where(low, split[1], split[0])
        return (keep.astype(F32) + swap(send, "pair").astype(F32)).astype(BF)

    def gather_chips(values):
        return lax.all_gather(values, CHIPS, axis=0)

    def scatter_chips(values):
        return lax.psum_scatter(values, CHIPS, scatter_dimension=0)

    def sum_chips(values):
        return pair_sum(pair_sum(values, "cy", 2), "cz", cz)

    def body(
        tokens,
        positions,
        cotangent,
        query_weight,
        key_weight,
        value_weight,
        out_weight,
        gate_weight,
        up_weight,
        down_weight,
        query_bias,
        key_bias,
        value_bias,
        first_gain,
        second_gain,
    ):
        core0 = lax.axis_index("core") == 0
        pair = lax.axis_index("pair")
        quarter = 2 * lax.axis_index("cy") + lax.axis_index("core")
        seqs, run, width = tokens.shape
        rows = seqs * run
        ff = gate_weight.shape[1]
        part = down_weight.shape[0]
        window = min(part, -(-part // 512) * 128)
        begins = [min(q * window, part - window) for q in range(4)]
        skips = [min(q * window - begins[q], window) for q in range(4)]
        slab = gate_weight.shape[0]

        def heads_of(values, each):
            return jnp.where(core0, values[..., :each], values[..., each:])

        turned = Q_WIDTH + HEAD_DIM
        kv_rows = key_bias.shape[0]
        vectors = jnp.concatenate([query_bias, key_bias, value_bias, first_gain, second_gain])
        lanes = vectors.shape[0]
        wide = turned + HEAD_DIM
        lines = -(-lanes // wide)
        vectors = jnp.concatenate([vectors, jnp.zeros((16 * wide - lanes,), BF)]).reshape(16, wide)
        qkv_local = jnp.concatenate(
            [
                jnp.concatenate(
                    [
                        heads_of(query_weight, Q_WIDTH),
                        heads_of(key_weight, HEAD_DIM),
                        heads_of(value_weight, HEAD_DIM),
                    ],
                    axis=1,
                ),
                vectors,
            ]
        )
        tokens_far = swap(tokens, "core")
        def by_quarter(choices):
            out = choices[3]
            for q in range(3):
                out = jnp.where(quarter == q, choices[q], out)
            return out

        def columns(values, q):
            at = [owner * part + begins[q] for owner in range(owners)]
            return jnp.concatenate([values[:, a : a + window] for a in at], axis=1)

        inside = lax.broadcasted_iota(jnp.int32, (1, owners * window), 1) % window
        skip = by_quarter([jnp.int32(n) for n in skips])

        def units(values):
            full = by_quarter([columns(values, q) for q in range(4)])
            return jnp.where(inside < skip, jnp.zeros((), BF), full)

        gate_own = units(gate_weight)
        up_own = units(up_weight)
        down_own = by_quarter([down_weight[at : at + window] for at in begins])
        qkv_all = gather_rows(qkv_local)
        qkv_all, gate_own, up_own, out_own, down_own = lax.optimization_barrier(
            (qkv_all, gate_own, up_own, out_weight, down_own)
        )
        qkv_all = qkv_all.reshape(owners, slab + 16, wide)
        qkv = qkv_all[:, :slab].reshape(owners * slab, wide)
        vectors = qkv_all[:, slab:].reshape(owners, -1)

        def vector_of(at, size):
            return vectors[:, at : at + size].reshape(-1)

        qb = vector_of(0, slab)
        kb = vector_of(slab, kv_rows)
        vb = vector_of(slab + kv_rows, kv_rows)
        fgain = vector_of(slab + 2 * kv_rows, slab).astype(F32)
        sgain = vector_of(2 * slab + 2 * kv_rows, slab).astype(F32)
        bias = jnp.concatenate(
            [heads_of(qb, Q_WIDTH), heads_of(kb, HEAD_DIM), heads_of(vb, HEAD_DIM)]
        ).astype(F32)[None]
        out_full = gather_rows(out_own)
        out_w = jnp.where(core0, out_full[:Q_WIDTH], out_full[Q_WIDTH:])
        down_w = gather_rows(down_own)
        gate_w = gather_rows(gate_own)
        up_w = gather_rows(up_own)

        places = jnp.stack([positions, swap(positions, "core")])
        firsts = places[:, :, ::BLK]
        starts = gather_small(gather_small(firsts, "cy", 2), "cz", cz)
        starts = starts.transpose(3, 0, 1, 2, 4).reshape(seqs, -1)
        qpos = places.transpose(1, 0, 2).reshape(seqs, 1, 2 * run)
        freq = theta ** (-jnp.arange(HALF, dtype=F32) / HALF)
        angles = places.reshape(2 * rows, 1).astype(F32) * freq
        cosine, sine = jnp.cos(angles), jnp.sin(angles)
        cos_wide = jnp.concatenate([cosine] * 4, axis=1)
        sin_wide = jnp.concatenate([-sine, sine] * 2, axis=1)

        def turned_rows(table):
            table = table.reshape(2, seqs, run, HALF).transpose(1, 3, 0, 2)
            return table.reshape(seqs, HALF, 2 * run)

        own_rows = tokens.reshape(rows, width)
        chip_rows = jnp.concatenate([own_rows, tokens_far.reshape(rows, width)])
        first, q, kv = project(
            chip_rows, fgain[None], qkv, bias, cos_wide, sin_wide
        )
        q = q.reshape(2, seqs, run, Q_WIDTH)
        kv = kv.reshape(2, seqs, run, 2 * HEAD_DIM)
        cut = seqs // 2
        kv_all = gather_chips(kv)
        kv_all, out_w, down_w, gate_w, cot_late = lax.optimization_barrier(
            (kv_all, out_w, down_w, gate_w, cotangent)
        )
        grad_own = cot_late.reshape(rows, width)
        far_grad = swap(grad_own, "cy")
        attn, lse = attention(False, 0, seqs, starts, qpos, q, kv_all)
        attn_rows = attn.reshape(2 * rows, Q_WIDTH)
        attn_rows, up_w, far_grad = lax.optimization_barrier((attn_rows, up_w, far_grad))
        attn_part = dot(attn_rows, out_w).astype(BF)
        inputs = own_rows.astype(F32)
        middle = (
            inputs
            + attn_part[:rows].astype(F32)
            + swap(attn_part[rows:], "core").astype(F32)
        )

        second = rms_scale(middle, sgain).astype(BF)
        near_c = jnp.concatenate([grad_own, swap(grad_own, "core")])
        far_c = jnp.concatenate([far_grad, swap(far_grad, "core")])
        far_second = swap(second, "cy")
        near_s = jnp.concatenate([second, swap(second, "core")])
        near_h, near_g, near_u, near_mix, near_gs = mlp(near_s, near_c, gate_w, up_w, down_w)
        far_second, near_h, near_g, near_u, near_mix, near_gs = lax.optimization_barrier(
            (far_second, near_h, near_g, near_u, near_mix, near_gs)
        )
        far_s = jnp.concatenate([far_second, swap(far_second, "core")])
        far_h, far_g, far_u, far_mix, far_gs = mlp(far_s, far_c, gate_w, up_w, down_w)

        def sum_back(near, far):
            far_own = far[:rows].astype(F32) + swap(far[rows:], "core").astype(F32)
            near_own = near[:rows].astype(F32) + swap(near[rows:], "core").astype(F32)
            return near_own + swap(far_own.astype(BF), "cy").astype(F32)

        grad_second = sum_back(near_gs, far_gs)
        near_gs, far_gs, near_g, near_u, near_h = lax.optimization_barrier(
            (near_gs, far_gs, near_g, near_u, near_h)
        )
        grad_down_w = weight_grad((near_h, near_c), (far_h, far_c))
        grad_gate_w = weight_grad((near_s, near_g), (far_s, far_g))
        grad_up_w = weight_grad((near_s, near_u), (far_s, far_u))
        sums = [sum_owners(values) for values in (grad_down_w, grad_gate_w, grad_up_w)]
        each = slab // cz
        line = jnp.concatenate([v.reshape(cz, each, owners * window) for v in sums], axis=1)

        _, pull_second = jax.vjp(rms_scale, middle, sgain)
        grad_middle_part, grad_sgain = pull_second(grad_second)
        grad_middle = grad_own.astype(F32) + grad_middle_part
        grad_branch = grad_middle.astype(BF)
        grad_branch = jnp.concatenate([grad_branch, swap(grad_branch, "core")])
        grad_out_w = dot(attn_rows, grad_branch, TN).astype(BF)
        grad_attn = dot(grad_branch, out_w, NT).astype(BF).reshape(2, seqs, run, Q_WIDTH)

        cos_t, sin_t = turned_rows(cosine), turned_rows(sine)

        arrived = None
        parts = []
        for step in range(cz - 1):
            loads = line_load(line, "cz", step, arrived)
            if step < 2:
                loads, grad_attn = lax.optimization_barrier((loads, grad_attn))
                grad_q_part, grad_kv_part = attention(
                    True,
                    step * cut,
                    seqs - cut if step else cut,
                    starts,
                    qpos,
                    q,
                    kv_all,
                    grad_attn,
                    lse,
                    cos_t,
                    sin_t,
                )
            arrived = line_send(loads, "cz", cz, step)
            if step < 2:
                grad_q_part, grad_kv_part, arrived = lax.optimization_barrier(
                    (grad_q_part, grad_kv_part, arrived)
                )
                parts.append((grad_q_part, scatter_chips(grad_kv_part)))
        (grad_q_near, grad_kv_near), (grad_q_far, grad_kv_far) = parts
        grad_q_near, near_mix, far_mix = lax.optimization_barrier((grad_q_near, near_mix, far_mix))
        mixed = (middle + sum_back(near_mix, far_mix)).astype(BF).reshape(seqs, run, width)
        grad_q = jnp.concatenate([grad_q_near, grad_q_far], axis=1).reshape(2 * rows, Q_WIDTH)
        grad_q_w = dot(first, grad_q, TN).astype(BF)
        grad_kv = jnp.concatenate([grad_kv_near, grad_kv_far], axis=1)
        grad_kv = grad_kv.reshape(2 * rows, 2 * HEAD_DIM).astype(F32)
        front = grad_kv[:, :HALF]
        back = grad_kv[:, HALF:HEAD_DIM]
        grad_kv = jnp.concatenate(
            [front * cosine + back * sine, back * cosine - front * sine, grad_kv[:, HEAD_DIM:]],
            axis=1,
        ).astype(BF)
        grad_qkv = jnp.concatenate([grad_q, grad_kv], axis=1)
        grad_kv_w = dot(first, grad_kv, TN).astype(BF)
        grad_biases = jnp.sum(grad_qkv.astype(F32), axis=0)
        grad_first_part = dot(grad_qkv, qkv, NT).astype(BF)
        grad_first = grad_first_part[:rows].astype(F32) + swap(
            grad_first_part[rows:], "core"
        ).astype(F32)
        _, pull_first = jax.vjp(rms_scale, inputs, fgain)
        grad_input_part, grad_fgain = pull_first(grad_first)
        grad_tokens = (grad_middle + grad_input_part).reshape(seqs, run, width)

        mine = line_total(line, "cz", arrived)
        mine_down = line_gather(mine[:each], "cz", cz).reshape(window, width)
        near, far = ordered("cy", mine_down, swap(mine_down, "cy"))
        both = jnp.stack([near, far])
        low, high = ordered("core", both, swap(both, "core"))
        down_parts = [low[0], high[0], low[1], high[1]]
        out_down = jnp.concatenate(
            [w[n:] for w, n in zip(down_parts, skips) if n < window]
        ).astype(F32)

        def full_columns(values):
            every = lax.all_gather(values, CHIPS + ("core",), axis=0)
            every = every.reshape(cz, 4, each, owners * window)
            pieces = [
                every[:, q, :, owner * window + skips[q] : (owner + 1) * window]
                for owner in range(owners)
                for q in range(4)
                if skips[q] < window
            ]
            return jnp.concatenate(pieces, axis=2).reshape(slab, ff).astype(F32)

        out_gate = full_columns(mine[each : 2 * each])
        out_up = full_columns(mine[2 * each :])

        def own_rows_of(values):
            return sum_chips(sum_owners(values))

        def both_cores(values):
            return [v.astype(F32) for v in ordered("core", values, swap(values, "core"))]

        all_out = jnp.concatenate(ordered("core", grad_out_w, swap(grad_out_w, "core")))
        early = sum_owners(jnp.concatenate([all_out, grad_q_w], axis=1))
        early = jnp.concatenate(
            [heads_of(early[:, :width], width // 2), early[:, width:]], axis=1
        )
        low_early, high_early = both_cores(sum_chips(early))
        out_out = jnp.concatenate([low_early[:, : width // 2], high_early[:, : width // 2]], axis=1)
        out_query = jnp.concatenate(
            [low_early[:, width // 2 :], high_early[:, width // 2 :]], axis=1
        )
        low_kv, high_kv = both_cores(own_rows_of(grad_kv_w))
        out_key = jnp.concatenate([low_kv[:, :HEAD_DIM], high_kv[:, :HEAD_DIM]], axis=1)
        out_value = jnp.concatenate([low_kv[:, HEAD_DIM:], high_kv[:, HEAD_DIM:]], axis=1)

        zeros = jnp.zeros((), F32)

        def spread(values):
            return jnp.concatenate(
                [jnp.where(core0, values, zeros), jnp.where(core0, zeros, values)]
            )

        vector = jnp.concatenate(
            [
                spread(grad_biases[:Q_WIDTH]),
                spread(grad_biases[Q_WIDTH:turned]),
                spread(grad_biases[turned:]),
                grad_fgain,
                grad_sgain,
            ]
        )
        vector = pair_sum(pair_sum(sum_chips(vector), "core", CORES), "pair", 2)
        if outer > 1:
            vector = pair_sum(vector, "outer", outer)
        owner = 2 * lax.axis_index("outer") + pair
        vectors = []
        at = 0
        for size in (width, KV_HEADS * HEAD_DIM, KV_HEADS * HEAD_DIM, width, width):
            each = size // owners
            vectors.append(lax.dynamic_slice(vector, (at + owner * each,), (each,)))
            at += size
        return (
            mixed,
            grad_tokens,
            out_query,
            out_key,
            out_value,
            out_out,
            out_gate,
            out_up,
            out_down,
            *vectors,
        )

    return body


def solution(mesh):
    ctx, fsdp = mesh.shape["ctx"], mesh.shape["fsdp"]
    sizes = {"cz": ctx // (2 * CORES), "cy": 2, "core": CORES, "outer": fsdp // 2, "pair": 2}
    fine = Mesh(mesh.devices.reshape(tuple(sizes.values())), tuple(sizes))
    ctx_axes = ("cz", "cy", "core")
    fsdp_axes = ("outer", "pair")
    in_specs = (
        P(fsdp_axes, ctx_axes, None),
        P(fsdp_axes, ctx_axes),
        P(fsdp_axes, ctx_axes, None),
        *[P(fsdp_axes, None)] * 7,
        *[P(fsdp_axes)] * 5,
    )
    out_specs = (
        P(fsdp_axes, ctx_axes, None),
        P(fsdp_axes, ctx_axes, None),
        *[P(fsdp_axes, None)] * 7,
        *[P(fsdp_axes)] * 5,
    )
    return jax.shard_map(
        make_body(sizes), mesh=fine, in_specs=in_specs, out_specs=out_specs, check_vma=False
    )
```

```python
import functools

import jax
import jax.numpy as jnp
from jax import lax
from jax.experimental import pallas as pl
from jax.experimental.pallas import tpu as pltpu
from jax.sharding import Mesh, PartitionSpec as P

Q_HEADS = 14
KV_HEADS = 2
HEAD_DIM = 64
GROUP = Q_HEADS // KV_HEADS
HALF = HEAD_DIM // 2
BLK = 32
CORES = 2
Q_WIDTH = GROUP * HEAD_DIM

epsilon = 1e-06
theta = 1000000.0
scale = HEAD_DIM ** (-0.5)

BF = jnp.bfloat16
F32 = jnp.float32
CHIPS = ("cz", "cy")
VMEM = 56 * 1024 * 1024
SWAP = [(0, 1), (1, 0)]
NT = (((1,), (1,)), ((), ()))
TN = (((0,), (0,)), ((), ()))


def swap(values, axis):
    return lax.ppermute(values, axis, SWAP)


def dot(left, right, dims=(((1,), (0,)), ((), ()))):
    return lax.dot_general(left, right, dims, preferred_element_type=F32)


def rms_scale(rows, gain):
    inverse = lax.rsqrt(jnp.mean(rows * rows, axis=-1, keepdims=True) + epsilon)
    return rows * inverse * gain


def project_kernel(x_ref, gain_ref, w_ref, b_ref, cos_ref, sin_ref, first_ref, q_ref, kv_ref):
    rows = x_ref[...].astype(F32)
    first = rms_scale(rows, gain_ref[...]).astype(BF)
    first_ref[...] = first
    pre = dot(first, w_ref[...]) + b_ref[...]
    turned = Q_WIDTH + HEAD_DIM
    cosine = jnp.concatenate([cos_ref[...]] * (turned // 128), axis=1)
    sine = jnp.concatenate([sin_ref[...]] * (turned // 128), axis=1)
    front = pre[:, :turned]
    lane = lax.broadcasted_iota(jnp.int32, front.shape, 1) % HEAD_DIM
    other = jnp.where(
        lane < HALF, pltpu.roll(front, turned - HALF, 1), pltpu.roll(front, HALF, 1)
    )
    rot = front * cosine + other * sine
    q_ref[...] = (rot[:, :Q_WIDTH] * scale).astype(BF)
    kv_ref[...] = jnp.concatenate([rot[:, Q_WIDTH:], pre[:, turned:]], axis=1).astype(BF)


def project(rows, gain, weight, bias, cosine, sine):
    count, width = rows.shape
    wide = weight.shape[1]
    step = 256
    row_block = lambda n: pl.BlockSpec((step, n), lambda i: (i, 0))
    whole = lambda a, b: pl.BlockSpec((a, b), lambda i: (0, 0))
    return pl.pallas_call(
        project_kernel,
        grid=(count // step,),
        in_specs=[
            row_block(width),
            whole(1, width),
            whole(width, wide),
            whole(1, wide),
            row_block(128),
            row_block(128),
        ],
        out_specs=[row_block(width), row_block(Q_WIDTH), row_block(2 * HEAD_DIM)],
        out_shape=[
            jax.ShapeDtypeStruct((count, width), BF),
            jax.ShapeDtypeStruct((count, Q_WIDTH), BF),
            jax.ShapeDtypeStruct((count, 2 * HEAD_DIM), BF),
        ],
        compiler_params=pltpu.CompilerParams(vmem_limit_bytes=VMEM),
        cost_estimate=pl.CostEstimate(
            flops=2 * count * width * wide, bytes_accessed=count * width * 4, transcendentals=0
        ),
    )(rows, gain, weight, bias, cosine, sine)


def stack_heads(flat):
    return jnp.concatenate(
        [flat[:, h * HEAD_DIM : (h + 1) * HEAD_DIM] for h in range(GROUP)], axis=0
    )


def fill_bias(offset, starts_ref, qpos_ref, bias_ref):
    own = qpos_ref[0]
    inside = lax.broadcasted_iota(jnp.int32, (BLK, own.shape[1]), 0)
    seq = pl.program_id(0) + offset
    for j in range(bias_ref.shape[0] // BLK):
        far = inside + starts_ref[seq, j]
        bias_ref[j * BLK : (j + 1) * BLK, :] = jnp.where(far <= own, 0.0, -1e30)


def query_chunks(local):
    total = GROUP * local
    return [(lo, min(lo + 2 * local, total)) for lo in range(0, total, 2 * local)]


def attend_kernel(offset, starts_ref, qpos_ref, q_ref, kv_ref, o_ref, lse_ref, bias_ref):
    local = 2 * q_ref.shape[2]
    keys = bias_ref.shape[0]
    fill_bias(offset, starts_ref, qpos_ref, bias_ref)
    kv = kv_ref[...].reshape(keys, 2 * HEAD_DIM)
    key = kv[:, :HEAD_DIM]
    value_t = kv.astype(F32).T[HEAD_DIM:].astype(BF)
    query = stack_heads(q_ref[...].reshape(local, Q_WIDTH))
    heads = []
    for lo, hi in query_chunks(local):
        bias = jnp.concatenate([bias_ref[...]] * ((hi - lo) // local), axis=1)
        scores = dot(key, query[lo:hi], NT) + bias
        top = jnp.max(scores, axis=0, keepdims=True)
        expo = jnp.exp(scores - top)
        total = jnp.sum(expo, axis=0, keepdims=True)
        out = dot(value_t, expo.astype(BF)) / total
        lse_ref[0, :, lo:hi] = top + jnp.log(total)
        heads += [out[:, at : at + local].T for at in range(0, hi - lo, local)]
    o_ref[...] = jnp.concatenate(heads, axis=1).astype(BF).reshape(o_ref.shape)


def attend_back_kernel(
    offset,
    starts_ref,
    qpos_ref,
    q_ref,
    kv_ref,
    do_ref,
    lse_ref,
    cos_ref,
    sin_ref,
    dq_ref,
    dkv_ref,
    bias_ref,
    probs_ref,
    grads_ref,
):
    local = 2 * q_ref.shape[2]
    keys = bias_ref.shape[0]
    fill_bias(offset, starts_ref, qpos_ref, bias_ref)
    kv = kv_ref[...].reshape(keys, 2 * HEAD_DIM)
    key = kv[:, :HEAD_DIM]
    value = kv[:, HEAD_DIM:]
    key_t = kv.astype(F32).T[:HEAD_DIM].astype(BF)
    query = stack_heads(q_ref[...].reshape(local, Q_WIDTH))
    grad_o = stack_heads(do_ref[...].reshape(local, Q_WIDTH))
    cosine = cos_ref[0]
    sine = sin_ref[0]
    heads = []
    for lo, hi in query_chunks(local):
        bias = jnp.concatenate([bias_ref[...]] * ((hi - lo) // local), axis=1)
        scores = dot(key, query[lo:hi], NT) + bias
        probs = jnp.exp(scores - lse_ref[0, :, lo:hi])
        probs_ref[:, lo:hi] = probs.astype(BF)
        grad_p = dot(value, grad_o[lo:hi], NT)
        inner = jnp.sum(probs * grad_p, axis=0, keepdims=True)
        grad_s = (probs * (grad_p - inner)).astype(BF)
        grads_ref[:, lo:hi] = grad_s
        grad_q = dot(key_t, grad_s) * scale
        for at in range(0, hi - lo, local):
            front = grad_q[:HALF, at : at + local]
            back = grad_q[HALF:, at : at + local]
            turned = jnp.concatenate(
                [front * cosine + back * sine, back * cosine - front * sine], axis=0
            )
            heads.append(turned.T)
    dq_ref[...] = jnp.concatenate(heads, axis=1).astype(BF).reshape(dq_ref.shape)
    grad_k = dot(grads_ref[...], query)
    grad_v = dot(probs_ref[...], grad_o)
    dkv_ref[...] = jnp.concatenate([grad_k, grad_v], axis=1).astype(BF).reshape(dkv_ref.shape)


def attention(back, offset, seqs, starts, qpos, q, kv, *more):
    run = q.shape[2]
    chips = kv.shape[0]
    local = 2 * run
    keys = chips * local
    total = GROUP * local
    q_spec = pl.BlockSpec((2, 1, run, Q_WIDTH), lambda s, st: (0, s + offset, 0, 0))
    part_spec = pl.BlockSpec((2, 1, run, Q_WIDTH), lambda s, st: (0, s, 0, 0))
    kv_block = (chips, 2, 1, run, 2 * HEAD_DIM)
    kv_spec = pl.BlockSpec(kv_block, lambda s, st: (0, 0, s + offset, 0, 0))
    kv_part_spec = pl.BlockSpec(kv_block, lambda s, st: (0, 0, s, 0, 0))
    lse_spec = pl.BlockSpec((1, 1, total), lambda s, st: (s + offset, 0, 0))
    qpos_spec = pl.BlockSpec((1, 1, local), lambda s, st: (s + offset, 0, 0))
    turn_spec = pl.BlockSpec((1, HALF, local), lambda s, st: (s + offset, 0, 0))
    in_specs = [qpos_spec, q_spec, kv_spec]
    scratch = [pltpu.VMEM((keys, local), F32)]
    part_shape = jax.ShapeDtypeStruct((2, seqs, run, Q_WIDTH), BF)
    if back:
        in_specs += [q_spec, lse_spec, turn_spec, turn_spec]
        out_specs = [part_spec, kv_part_spec]
        kv_shape = kv.shape[:2] + (seqs,) + kv.shape[3:]
        out_shape = [part_shape, jax.ShapeDtypeStruct(kv_shape, BF)]
        scratch += [pltpu.VMEM((keys, total), BF)] * 2
    else:
        out_specs = [part_spec, lse_spec]
        out_shape = [part_shape, jax.ShapeDtypeStruct((seqs, 1, total), F32)]
    passes = 5 if back else 2
    return pl.pallas_call(
        functools.partial(attend_back_kernel if back else attend_kernel, offset),
        grid_spec=pltpu.PrefetchScalarGridSpec(
            num_scalar_prefetch=1,
            grid=(seqs,),
            in_specs=in_specs,
            out_specs=out_specs,
            scratch_shapes=scratch,
        ),
        out_shape=out_shape,
        compiler_params=pltpu.CompilerParams(vmem_limit_bytes=VMEM),
        cost_estimate=pl.CostEstimate(
            flops=8 * passes * seqs * keys * total * HEAD_DIM,
            bytes_accessed=seqs * keys * 512,
            transcendentals=seqs * keys * total,
        ),
    )(starts, qpos, q, kv, *more)


def mlp_kernel(s_ref, c_ref, g_ref, u_ref, d_ref, hid_ref, gg_ref, gu_ref, mix_ref, gs_ref):
    rows = s_ref[...]
    grad = c_ref[...]
    wide = g_ref.shape[1]
    for lo in range(0, wide, 256):
        hi = min(lo + 256, wide)
        gate = dot(rows, g_ref[:, lo:hi])
        up = dot(rows, u_ref[:, lo:hi])
        grad_hidden = dot(grad, d_ref[lo:hi, :], NT)
        sig = 1.0 / (1.0 + jnp.exp(-gate))
        silu = gate * sig
        hid_ref[:, lo:hi] = (silu * up).astype(BF)
        gg_ref[:, lo:hi] = (grad_hidden * up * (sig * (1.0 + gate * (1.0 - sig)))).astype(BF)
        gu_ref[:, lo:hi] = (grad_hidden * silu).astype(BF)
    mix_ref[...] = dot(hid_ref[...], d_ref[...]).astype(BF)
    gs_ref[...] = (dot(gg_ref[...], g_ref[...], NT) + dot(gu_ref[...], u_ref[...], NT)).astype(BF)


def mlp(rows, grad, gate_w, up_w, down_w):
    count, width = rows.shape
    wide = gate_w.shape[1]
    step = 256
    row_block = lambda n: pl.BlockSpec((step, n), lambda i: (i, 0))
    whole = lambda a, b: pl.BlockSpec((a, b), lambda i: (0, 0))
    shape = lambda n: jax.ShapeDtypeStruct((count, n), BF)
    return pl.pallas_call(
        mlp_kernel,
        grid=(count // step,),
        in_specs=[
            row_block(width),
            row_block(width),
            whole(width, wide),
            whole(width, wide),
            whole(wide, width),
        ],
        out_specs=[row_block(wide)] * 3 + [row_block(width)] * 2,
        out_shape=[shape(wide)] * 3 + [shape(width)] * 2,
        compiler_params=pltpu.CompilerParams(vmem_limit_bytes=VMEM),
        cost_estimate=pl.CostEstimate(
            flops=12 * count * width * wide,
            bytes_accessed=count * (wide * 6 + width * 8),
            transcendentals=count * wide,
        ),
    )(rows, grad, gate_w, up_w, down_w)


def weight_grad_kernel(pair_ref, a_near, a_far, b_near, b_far, keep_ref, send_ref, acc_ref):
    step = pl.program_id(0)
    steps = pl.num_programs(0)

    @pl.when(step == 0)
    def _():
        acc_ref[...] = dot(a_near[...], b_near[...], TN)

    @pl.when(jnp.logical_and(step > 0, step < steps // 2))
    def _():
        acc_ref[...] += dot(a_near[...], b_near[...], TN)

    @pl.when(step >= steps // 2)
    def _():
        acc_ref[...] += dot(a_far[...], b_far[...], TN)

    @pl.when(step == steps - 1)
    def _():
        outer, parts, tall, _ = keep_ref.shape
        tiles = acc_ref.shape[1] // 128
        high = tall // tiles
        slab = parts * high
        for out_ref, which in ((keep_ref, pair_ref[0]), (send_ref, 1 - pair_ref[0])):
            for o in range(outer):
                start = pl.multiple_of((2 * o + which) * slab, slab)
                for t in range(tiles):
                    tile = acc_ref[pl.ds(start, slab), t * 128 : (t + 1) * 128].astype(BF)
                    for z in range(parts):
                        out_ref[o, z, t * high : (t + 1) * high, :] = tile[
                            z * high : (z + 1) * high
                        ]


def weight_grad(pair, outer, parts, near, far):
    (a_near, b_near), (a_far, b_far) = near, far
    count, high = a_near.shape
    wide = b_near.shape[1]
    half = 2
    step = count // half
    tall = high // (2 * outer * parts) * (wide // 128)
    near_block = lambda n: pl.BlockSpec((step, n), lambda i, p: (jnp.minimum(i, half - 1), 0))
    far_block = lambda n: pl.BlockSpec((step, n), lambda i, p: (jnp.maximum(i - half, 0), 0))
    out_spec = pl.BlockSpec((outer, parts, tall, 128), lambda i, p: (0, 0, 0, 0))
    shape = jax.ShapeDtypeStruct((outer, parts, tall, 128), BF)
    return pl.pallas_call(
        weight_grad_kernel,
        grid_spec=pltpu.PrefetchScalarGridSpec(
            num_scalar_prefetch=1,
            grid=(2 * half,),
            in_specs=[near_block(high), far_block(high), near_block(wide), far_block(wide)],
            out_specs=[out_spec, out_spec],
            scratch_shapes=[pltpu.VMEM((high, wide), F32)],
        ),
        out_shape=[shape, shape],
        compiler_params=pltpu.CompilerParams(vmem_limit_bytes=VMEM),
        cost_estimate=pl.CostEstimate(
            flops=4 * count * high * wide,
            bytes_accessed=4 * count * (high + wide),
            transcendentals=0,
        ),
    )(pair, a_near, a_far, b_near, b_far)


def spread_rows_kernel(skip, in_ref, out_ref):
    parts, windows, _, tall, _ = in_ref.shape
    tiles = out_ref.shape[1] // 128
    high = tall // tiles
    for q in range(windows):
        drop = skip if q == windows - 1 else 0
        for z in range(parts):
            lo = max(drop - z * high, 0)
            if lo >= high:
                continue
            at = q * parts * high + z * high + lo - drop
            for t in range(tiles):
                out_ref[at : at + high - lo, t * 128 : (t + 1) * 128] = in_ref[
                    z, q, 0, t * high + lo : (t + 1) * high, :
                ].astype(F32)


def spread_rows(every, skip, part):
    parts, windows, _, tall, _ = every.shape
    width = tall * parts * 128 // ((part + skip) // windows)
    return pl.pallas_call(
        functools.partial(spread_rows_kernel, skip),
        grid=(1,),
        in_specs=[pl.BlockSpec((parts, windows, 1, tall, 128), lambda i: (0, 0, 0, 0, 0))],
        out_specs=pl.BlockSpec((part, width), lambda i: (0, 0)),
        out_shape=jax.ShapeDtypeStruct((part, width), F32),
        compiler_params=pltpu.CompilerParams(vmem_limit_bytes=VMEM),
    )(every)


def spread_columns_kernel(owners, part, begins, skips, gate_ref, up_ref, gate_out, up_out):
    high = gate_out.shape[0]
    tiles = gate_ref.shape[3] // high // owners
    for in_ref, out_ref in ((gate_ref, gate_out), (up_ref, up_out)):
        for owner in range(owners):
            for q in range(4):
                for t in range(skips[q] // 128, tiles):
                    at = owner * part + begins[q] + 128 * t
                    row = (owner * tiles + t) * high
                    out_ref[:, at : at + 128] = in_ref[0, q, 0, row : row + high, :].astype(F32)


def spread_columns(every, owners, part, begins, skips):
    parts, _, _, tall, _ = every.shape
    window = part - begins[3]
    high = tall * 128 // (owners * window)
    block = (1, 4, 1, tall, 128)
    out_spec = pl.BlockSpec((high, owners * part), lambda z: (z, 0))
    shape = jax.ShapeDtypeStruct((parts * high, owners * part), F32)
    return pl.pallas_call(
        functools.partial(spread_columns_kernel, owners, part, begins, skips),
        grid=(parts,),
        in_specs=[
            pl.BlockSpec(block, lambda z: (z, 0, 1, 0, 0)),
            pl.BlockSpec(block, lambda z: (z, 0, 2, 0, 0)),
        ],
        out_specs=[out_spec, out_spec],
        out_shape=[shape, shape],
        compiler_params=pltpu.CompilerParams(vmem_limit_bytes=VMEM),
    )(every, every)


def gather_small(values, axis, size):
    out = values[None]
    index = lax.axis_index(axis)
    bit = 1
    while bit < size:
        other = lax.ppermute(out, axis, [(i, i ^ bit) for i in range(size)])
        low = (index & bit) == 0
        out = jnp.where(
            low, jnp.concatenate([out, other], axis=0), jnp.concatenate([other, out], axis=0)
        )
        bit *= 2
    return out


def line_part(values, at):
    at = jnp.clip(at, 0, values.shape[0] - 1)
    return lax.dynamic_index_in_dim(values, at, 0, keepdims=False).astype(F32)


def line_load(values, axis, step, arrived):
    size = values.shape[0]
    index = lax.axis_index(axis)
    far = size - 1 - step
    up, down = line_part(values, index + far), line_part(values, index - far)
    if step:
        up, down = up + arrived[0].astype(F32), down + arrived[1].astype(F32)
    return up.astype(BF), down.astype(BF)


def line_send(load, axis, size, step):
    far = size - 1 - step
    right = [(i, i + 1) for i in range(size - 1) if i <= step]
    left = [(i + 1, i) for i in range(size - 1) if i + 1 >= far]
    return lax.ppermute(load[0], axis, right), lax.ppermute(load[1], axis, left)


def line_total(values, axis, arrived):
    own = line_part(values, lax.axis_index(axis))
    return (own + arrived[0].astype(F32) + arrived[1].astype(F32)).astype(BF)


def line_gather(values, axis, size):
    index = lax.axis_index(axis)
    right = left = values
    rights, lefts = [], []
    for step in range(size - 1):
        right = lax.ppermute(right, axis, [(i, i + 1) for i in range(size - 1) if i >= step])
        left = lax.ppermute(
            left, axis, [(i + 1, i) for i in range(size - 1) if i + 1 <= size - 1 - step]
        )
        rights.append(right)
        lefts.append(left)
    row = jnp.stack(rights[::-1] + [values] + lefts)
    return lax.dynamic_slice_in_dim(row, size - 1 - index, size, 0)


def pair_sum(values, axis, size):
    bit = 1
    while bit < size:
        other = lax.ppermute(values, axis, [(i, i ^ bit) for i in range(size)])
        values = (values.astype(F32) + other.astype(F32)).astype(values.dtype)
        bit *= 2
    return values


def together(*values):
    return lax.optimization_barrier(values)


def make_body(sizes):
    cz, outer = sizes["cz"], sizes["outer"]
    chips = cz * sizes["cy"]
    owners = 2 * outer

    def ordered(axis, own, other):
        low = lax.axis_index(axis) == 0
        return jnp.where(low, own, other), jnp.where(low, other, own)

    def gather_rows(values):
        rows = values.shape[0]
        if outer > 1:
            values = lax.all_gather(values, "outer", axis=0)
        else:
            values = values[None]
        both = jnp.stack(ordered("pair", values, swap(values, "pair")), axis=1)
        return both.reshape((owners * rows,) + values.shape[2:])

    def gather_start(values):
        if outer > 1:
            values = lax.all_gather(values, "outer", axis=0)
        else:
            values = values[None]
        return swap(values, "pair")

    def gather_finish(values, far):
        if outer > 1:
            values = lax.all_gather(values, "outer", axis=0)
        else:
            values = values[None]
        both = jnp.stack(ordered("pair", values, far), axis=1)
        return both.reshape((owners * values.shape[1],) + values.shape[2:])

    def gather_chips(values):
        return lax.all_gather(values, CHIPS, axis=0)

    def split_cy(values, axis):
        half = values.shape[axis] // 2
        first = lax.slice_in_dim(values, 0, half, axis=axis)
        last = lax.slice_in_dim(values, half, 2 * half, axis=axis)
        low = lax.axis_index("cy") == 0
        return jnp.where(low, first, last), jnp.where(low, last, first)

    def split_owners(values):
        split = values.reshape(outer, 2, -1, values.shape[1])
        if outer > 1:
            split = lax.psum_scatter(split, "outer", scatter_dimension=0)
        else:
            split = split[0]
        low = lax.axis_index("pair") == 0
        return jnp.where(low, split[0], split[1]), jnp.where(low, split[1], split[0])

    def add(left, right):
        return (left.astype(F32) + right.astype(F32)).astype(left.dtype)

    def bits_of(size):
        return [1 << b for b in range((size - 1).bit_length())]

    def exchange(values, axis, size, bit):
        return lax.ppermute(values, axis, [(i, i ^ bit) for i in range(size)])

    def body(
        tokens,
        positions,
        cotangent,
        query_weight,
        key_weight,
        value_weight,
        out_weight,
        gate_weight,
        up_weight,
        down_weight,
        query_bias,
        key_bias,
        value_bias,
        first_gain,
        second_gain,
    ):
        core0 = lax.axis_index("core") == 0
        pair = lax.axis_index("pair")
        quarter = 2 * lax.axis_index("cy") + lax.axis_index("core")
        seqs, run, width = tokens.shape
        rows = seqs * run
        ff = gate_weight.shape[1]
        part = down_weight.shape[0]
        window = min(part, -(-part // 512) * 128)
        begins = [min(q * window, part - window) for q in range(4)]
        skips = [min(q * window - begins[q], window) for q in range(4)]
        slab = gate_weight.shape[0]

        def heads_of(values, each):
            return jnp.where(core0, values[..., :each], values[..., each:])

        places = jnp.stack([positions, swap(positions, "core")])
        firsts = places[:, :, ::BLK]
        starts = gather_small(gather_small(firsts, "cy", 2), "cz", cz)
        starts = starts.transpose(3, 0, 1, 2, 4).reshape(seqs, -1)
        qpos = places.transpose(1, 0, 2).reshape(seqs, 1, 2 * run)
        turned = Q_WIDTH + HEAD_DIM
        kv_rows = key_bias.shape[0]
        vectors = jnp.concatenate([query_bias, key_bias, value_bias, first_gain, second_gain])
        lanes = vectors.shape[0]
        wide = turned + HEAD_DIM
        lines = -(-lanes // wide)
        vectors = jnp.concatenate([vectors, jnp.zeros((16 * wide - lanes,), BF)]).reshape(16, wide)
        qkv_local = jnp.concatenate(
            [
                jnp.concatenate(
                    [
                        heads_of(query_weight, Q_WIDTH),
                        heads_of(key_weight, HEAD_DIM),
                        heads_of(value_weight, HEAD_DIM),
                    ],
                    axis=1,
                ),
                vectors,
            ]
        )
        tokens_far = swap(tokens, "core")
        def by_quarter(choices):
            out = choices[3]
            for q in range(3):
                out = jnp.where(quarter == q, choices[q], out)
            return out

        def columns(values, q):
            at = [owner * part + begins[q] for owner in range(owners)]
            return jnp.concatenate([values[:, a : a + window] for a in at], axis=1)

        inside = lax.broadcasted_iota(jnp.int32, (1, owners * window), 1) % window
        skip = by_quarter([jnp.int32(n) for n in skips])

        def units(values):
            full = by_quarter([columns(values, q) for q in range(4)])
            return jnp.where(inside < skip, jnp.zeros((), BF), full)

        gate_own = units(gate_weight)
        up_own = units(up_weight)
        down_own = by_quarter([down_weight[at : at + window] for at in begins])
        qkv_all = gather_rows(qkv_local)
        qkv_all, gate_own, up_own, out_own, down_own, starts, qpos = lax.optimization_barrier(
            (qkv_all, gate_own, up_own, out_weight, down_own, starts, qpos)
        )
        qkv_all = qkv_all.reshape(owners, slab + 16, wide)
        qkv = qkv_all[:, :slab].reshape(owners * slab, wide)
        vectors = qkv_all[:, slab:].reshape(owners, -1)

        def vector_of(at, size):
            return vectors[:, at : at + size].reshape(-1)

        qb = vector_of(0, slab)
        kb = vector_of(slab, kv_rows)
        vb = vector_of(slab + kv_rows, kv_rows)
        fgain = vector_of(slab + 2 * kv_rows, slab).astype(F32)
        sgain = vector_of(2 * slab + 2 * kv_rows, slab).astype(F32)
        bias = jnp.concatenate(
            [heads_of(qb, Q_WIDTH), heads_of(kb, HEAD_DIM), heads_of(vb, HEAD_DIM)]
        ).astype(F32)[None]
        if outer > 1:
            out_full = gather_rows(out_own)
            out_w = jnp.where(core0, out_full[:Q_WIDTH], out_full[Q_WIDTH:])
        else:
            out_far = lax.ppermute(out_own, ("core", "pair"), [(0, 1), (3, 2)])
            out_w = jnp.where(lax.axis_index("core") == pair, out_own, out_far)
        down_w = gather_rows(down_own)

        freq = theta ** (-jnp.arange(HALF, dtype=F32) / HALF)
        angles = places.reshape(2 * rows, 1).astype(F32) * freq
        cosine, sine = jnp.cos(angles), jnp.sin(angles)
        cos_wide = jnp.concatenate([cosine] * 4, axis=1)
        sin_wide = jnp.concatenate([-sine, sine] * 2, axis=1)

        def turned_rows(table):
            table = table.reshape(2, seqs, run, HALF).transpose(1, 3, 0, 2)
            return table.reshape(seqs, HALF, 2 * run)

        own_rows = tokens.reshape(rows, width)
        chip_rows = jnp.concatenate([own_rows, tokens_far.reshape(rows, width)])
        first, q, kv = project(
            chip_rows, fgain[None], qkv, bias, cos_wide, sin_wide
        )
        q = q.reshape(2, seqs, run, Q_WIDTH)
        kv = kv.reshape(2, seqs, run, 2 * HEAD_DIM)
        cut = seqs // 2
        kv_all = gather_chips(kv)
        gate_far = gather_start(gate_own)
        kv_all, out_w, down_w, cot_late, up_own = together(
            kv_all, out_w, down_w, cotangent, up_own
        )
        up_far = gather_start(up_own)
        grad_own = cot_late.reshape(rows, width)
        far_grad = swap(grad_own, "cy")
        attn, lse = attention(False, 0, seqs, starts, qpos, q, kv_all)
        attn_rows = attn.reshape(2 * rows, Q_WIDTH)
        attn_rows, gate_far, up_far, far_grad = together(attn_rows, gate_far, up_far, far_grad)
        gate_w = gather_finish(gate_own, gate_far)
        up_w = gather_finish(up_own, up_far)
        attn_part = dot(attn_rows, out_w).astype(BF)
        inputs = own_rows.astype(F32)
        middle = (
            inputs
            + attn_part[:rows].astype(F32)
            + swap(attn_part[rows:], "core").astype(F32)
        )

        second = rms_scale(middle, sgain).astype(BF)
        near_c = jnp.concatenate([grad_own, swap(grad_own, "core")])
        far_c = jnp.concatenate([far_grad, swap(far_grad, "core")])
        far_second = swap(second, "cy")
        near_s = jnp.concatenate([second, swap(second, "core")])
        near_h, near_g, near_u, near_mix, near_gs = mlp(near_s, near_c, gate_w, up_w, down_w)
        far_second, near_h, near_g, near_u, near_mix, near_gs = together(
            far_second, near_h, near_g, near_u, near_mix, near_gs
        )
        far_core, gs_core = together(swap(far_second, "core"), swap(near_gs[rows:], "core"))
        far_s = jnp.concatenate([far_second, far_core])
        far_h, far_g, far_u, far_mix, far_gs = mlp(far_s, far_c, gate_w, up_w, down_w)
        own_gs = near_gs[:rows].astype(F32) + gs_core.astype(F32)
        send_gs = add(far_gs[:rows], swap(far_gs[rows:], "core"))

        send_gs, far_h, far_g, far_u, far_mix = together(send_gs, far_h, far_g, far_u, far_mix)
        back_gs = swap(send_gs, "cy")
        pair_index = jnp.reshape(pair, (1,)).astype(jnp.int32)

        def unit_grad(near, far):
            keep, send = weight_grad(pair_index, outer, cz, near, far)
            if outer > 1:
                keep = lax.psum_scatter(keep, "outer", scatter_dimension=0)
                send = lax.psum_scatter(send, "outer", scatter_dimension=0)
                return keep, send
            return keep[0], send[0]

        keep_down, send_down = unit_grad((near_h, near_c), (far_h, far_c))
        keep_down, send_down, far_g, near_mix, far_mix = together(
            keep_down, send_down, far_g, near_mix, far_mix
        )
        sum_down = swap(send_down, "pair")
        mix_near_core = swap(near_mix[rows:], "core")
        mix_far_core = swap(far_mix[rows:], "core")
        keep_gate, send_gate = unit_grad((near_s, near_g), (far_s, far_g))
        keep_gate, far_u = together(keep_gate, far_u)
        keep_up, send_up = unit_grad((near_s, near_u), (far_s, far_u))
        keep_up, back_gs, sum_down, mix_near_core, mix_far_core, send_gate, send_up = together(
            keep_up, back_gs, sum_down, mix_near_core, mix_far_core, send_gate, send_up
        )
        sum_gate, sum_up = swap(send_gate, "pair"), swap(send_up, "pair")
        send_mix = add(far_mix[:rows], mix_far_core)
        back_mix = swap(send_mix, "cy")
        grad_second = own_gs + back_gs.astype(F32)
        _, pull_second = jax.vjp(rms_scale, middle, sgain)
        grad_middle_part, grad_sgain = pull_second(grad_second)
        grad_middle = grad_own.astype(F32) + grad_middle_part
        grad_branch = grad_middle.astype(BF)
        grad_branch = jnp.concatenate([grad_branch, swap(grad_branch, "core")])
        grad_attn = dot(grad_branch, out_w, NT).astype(BF).reshape(2, seqs, run, Q_WIDTH)
        grad_out_w = dot(attn_rows, grad_branch, TN).astype(BF)
        cos_t, sin_t = turned_rows(cosine), turned_rows(sine)

        def attend_back(at, count, grad):
            return attention(True, at, count, starts, qpos, q, kv_all, grad, lse, cos_t, sin_t)

        def keys_cy(values):
            return split_cy(values.reshape((cz, 2) + values.shape[1:]), 1)

        grad_q_near, grad_kv_near = attend_back(0, cut, grad_attn)
        grad_q_near, grad_kv_near, back_mix, sum_gate, sum_up = together(
            grad_q_near, grad_kv_near, back_mix, sum_gate, sum_up
        )
        mix_own = near_mix[:rows].astype(F32) + mix_near_core.astype(F32)
        mixed = (middle + mix_own + back_mix.astype(F32)).astype(BF).reshape(seqs, run, width)
        line = jnp.concatenate(
            [add(keep_down, sum_down), add(keep_gate, sum_gate), add(keep_up, sum_up)], axis=1
        )
        if outer > 1:
            every_out = jnp.concatenate(ordered("core", grad_out_w, swap(grad_out_w, "core")))
            keep_out, send_out = split_owners(every_out)
            out_rows = add(keep_out, swap(send_out, "pair"))
        else:
            far_out = lax.ppermute(grad_out_w, ("core", "pair"), [(1, 0), (2, 3)])
            out_rows = add(grad_out_w, far_out)
            mine_here = lax.axis_index("core") == pair
            out_rows = jnp.where(mine_here, out_rows, swap(out_rows, "core"))
        out_rows = heads_of(out_rows, width // 2)

        keep_near, send_near = keys_cy(grad_kv_near)
        load = line_load(line, "cz", 0, None)
        keep_out, send_out = split_cy(out_rows, 0)
        load, send_near, grad_late, send_out = together(load, send_near, grad_attn, send_out)
        far_out = swap(send_out, "cy")
        arrived = line_send(load, "cz", cz, 0)
        back_near = swap(send_near, "cy")
        grad_q_far, grad_kv_far = attend_back(cut, seqs - cut, grad_late)
        grad_q_far, grad_kv_far, arrived, back_near, far_out = together(
            grad_q_far, grad_kv_far, arrived, back_near, far_out
        )
        out_sum = add(keep_out, far_out)
        grad_q = jnp.concatenate([grad_q_near, grad_q_far], axis=1).reshape(2 * rows, Q_WIDTH)
        grad_q_w = dot(first, grad_q, TN).astype(BF)
        keep_far, send_far = keys_cy(grad_kv_far)
        keep_early, send_early = split_owners(grad_q_w)
        bits = bits_of(cz)
        load = line_load(line, "cz", 1, arrived)
        load, send_far, out_sum = together(load, send_far, out_sum)
        arrived, back_far, far_out = together(
            line_send(load, "cz", cz, 1),
            swap(send_far, "cy"),
            exchange(out_sum, "cz", cz, bits[0]),
        )
        out_sum = add(out_sum, far_out)
        keys = [add(keep_near, back_near), add(keep_far, back_far)]
        keys = jnp.concatenate(keys, axis=3).reshape(cz, 2 * rows, 2 * HEAD_DIM)
        load, keys_load = line_load(line, "cz", 2, arrived), line_load(keys, "cz", 0, None)
        load, keys_load, send_early, out_sum = together(load, keys_load, send_early, out_sum)
        arrived, keys_arrived, far_early, far_out = together(
            line_send(load, "cz", cz, 2),
            line_send(keys_load, "cz", cz, 0),
            swap(send_early, "pair"),
            exchange(out_sum, "cz", cz, bits[1]),
        )
        out_sum = add(out_sum, far_out)
        for bit in bits[2:]:
            out_sum = add(out_sum, exchange(out_sum, "cz", cz, bit))
        for step in range(3, cz - 1):
            arrived = line_send(line_load(line, "cz", step, arrived), "cz", cz, step)
        mine = line_total(line, "cz", arrived)
        early = add(keep_early, far_early)
        keep_early, send_early = split_cy(early, 0)
        keys_load = line_load(keys, "cz", 1, keys_arrived)
        mine, keys_load, send_early, out_sum = together(mine, keys_load, send_early, out_sum)
        keys_arrived, far_early, far_out = together(
            line_send(keys_load, "cz", cz, 1), swap(send_early, "cy"), swap(out_sum, "cy")
        )
        out_sum = jnp.concatenate(ordered("cy", out_sum, far_out))
        early = add(keep_early, far_early)
        for step in range(2, cz - 1):
            load = line_load(keys, "cz", step, keys_arrived)
            if step == 2:
                load, early, out_sum = together(load, early, out_sum)
                keys_arrived, far_early, far_sum = together(
                    line_send(load, "cz", cz, step),
                    exchange(early, "cz", cz, bits[0]),
                    swap(out_sum, "core"),
                )
                early = add(early, far_early)
            else:
                keys_arrived = line_send(load, "cz", cz, step)
        grad_kv = line_total(keys, "cz", keys_arrived).astype(F32)
        front = grad_kv[:, :HALF]
        back = grad_kv[:, HALF:HEAD_DIM]
        grad_kv = jnp.concatenate(
            [front * cosine + back * sine, back * cosine - front * sine, grad_kv[:, HEAD_DIM:]],
            axis=1,
        ).astype(BF)
        grad_qkv = jnp.concatenate([grad_q, grad_kv], axis=1)
        grad_kv_w = dot(first, grad_kv, TN).astype(BF)
        grad_biases = jnp.sum(grad_qkv.astype(F32), axis=0)
        grad_first_part = dot(grad_qkv, qkv, NT).astype(BF)
        keep_kv, send_kv = split_owners(grad_kv_w)
        for bit in bits[2:]:
            early = add(early, exchange(early, "cz", cz, bit))
        send_first, send_kv = together(grad_first_part[rows:], send_kv)
        far_early = exchange(early, "cz", cz, bits[1])
        far_first, far_kv = together(swap(send_first, "core"), swap(send_kv, "pair"))
        total_kv = add(keep_kv, far_kv)
        grad_first = grad_first_part[:rows].astype(F32) + far_first.astype(F32)
        _, pull_first = jax.vjp(rms_scale, inputs, fgain)
        grad_input_part, grad_fgain = pull_first(grad_first)
        grad_tokens = (grad_middle + grad_input_part).reshape(seqs, run, width)

        zeros = jnp.zeros((), F32)

        def spread(values):
            return jnp.concatenate(
                [jnp.where(core0, values, zeros), jnp.where(core0, zeros, values)]
            )

        vector = jnp.concatenate(
            [
                spread(grad_biases[:Q_WIDTH]),
                spread(grad_biases[Q_WIDTH:turned]),
                spread(grad_biases[turned:]),
                grad_fgain,
                grad_sgain,
            ]
        )
        hops = [("cz", cz, bit) for bit in bits] + [("cy", 2, 1)]
        for count, hop in enumerate(hops):
            total_kv, vector = together(total_kv, vector)
            last = count == len(hops) - 1
            sends = [exchange(total_kv, *hop), exchange(vector, *hop)] + [far_early] * last
            arrivals = together(*sends)
            total_kv, vector = add(total_kv, arrivals[0]), vector + arrivals[1]
            if last:
                early = add(early, arrivals[2])
        total_kv, vector = together(total_kv, vector)
        far_kv, far_vector, far_early = together(
            swap(total_kv, "core"), swap(vector, "core"), swap(early, "cy")
        )
        early = jnp.concatenate(ordered("cy", early, far_early))
        far_early = swap(early, "core")
        vector = vector + far_vector
        vector = pair_sum(vector, "pair", 2)
        if outer > 1:
            vector = pair_sum(vector, "outer", outer)
        out_query = jnp.concatenate(
            ordered("core", early.astype(F32), far_early.astype(F32)), axis=1
        )
        out_out = jnp.concatenate(
            ordered("core", out_sum.astype(F32), far_sum.astype(F32)), axis=1
        )
        low_kv, high_kv = ordered("core", total_kv.astype(F32), far_kv.astype(F32))
        out_key = jnp.concatenate([low_kv[:, :HEAD_DIM], high_kv[:, :HEAD_DIM]], axis=1)
        out_value = jnp.concatenate([low_kv[:, HEAD_DIM:], high_kv[:, HEAD_DIM:]], axis=1)
        owner = 2 * lax.axis_index("outer") + pair
        vectors = []
        at = 0
        for size in (width, KV_HEADS * HEAD_DIM, KV_HEADS * HEAD_DIM, width, width):
            share = size // owners
            vectors.append(lax.dynamic_slice(vector, (at + owner * share,), (share,)))
            at += size

        every = lax.all_gather(mine, CHIPS + ("core",), axis=0)
        every = every.reshape((cz, 4, 3, -1, 128))
        if part % 128 == 0 and not any(skips[:3]):
            out_down = spread_rows(every, skips[3], part)
            out_gate, out_up = spread_columns(every, owners, part, begins, skips)
        else:

            def windows(index, q, high):
                tiles = every[:, q, index].reshape(cz, -1, high // cz, 128)
                return tiles.transpose(0, 2, 1, 3).reshape(high, -1).astype(F32)

            out_down = jnp.concatenate(
                [windows(0, q, window)[skips[q] :] for q in range(4)]
            )

            def full_columns(index):
                pieces = [
                    windows(index, q, slab)[:, owner * window + skips[q] : (owner + 1) * window]
                    for owner in range(owners)
                    for q in range(4)
                ]
                return jnp.concatenate(pieces, axis=1)

            out_gate, out_up = full_columns(1), full_columns(2)
        return (
            mixed,
            grad_tokens,
            out_query,
            out_key,
            out_value,
            out_out,
            out_gate,
            out_up,
            out_down,
            *vectors,
        )

    return body


def solution(mesh):
    ctx, fsdp = mesh.shape["ctx"], mesh.shape["fsdp"]
    sizes = {"cz": ctx // (2 * CORES), "cy": 2, "core": CORES, "outer": fsdp // 2, "pair": 2}
    fine = Mesh(mesh.devices.reshape(tuple(sizes.values())), tuple(sizes))
    ctx_axes = ("cz", "cy", "core")
    fsdp_axes = ("outer", "pair")
    in_specs = (
        P(fsdp_axes, ctx_axes, None),
        P(fsdp_axes, ctx_axes),
        P(fsdp_axes, ctx_axes, None),
        *[P(fsdp_axes, None)] * 7,
        *[P(fsdp_axes)] * 5,
    )
    out_specs = (
        P(fsdp_axes, ctx_axes, None),
        P(fsdp_axes, ctx_axes, None),
        *[P(fsdp_axes, None)] * 7,
        *[P(fsdp_axes)] * 5,
    )
    return jax.shard_map(
        make_body(sizes), mesh=fine, in_specs=in_specs, out_specs=out_specs, check_vma=False
    )
```

```python
import functools

import jax
import jax.numpy as jnp
from jax import lax
from jax.experimental import pallas as pl
from jax.experimental.pallas import tpu as pltpu
from jax.sharding import Mesh, PartitionSpec as P

Q_HEADS = 14
KV_HEADS = 2
HEAD_DIM = 64
GROUP = Q_HEADS // KV_HEADS
HALF = HEAD_DIM // 2
BLK = 32
CORES = 2
Q_WIDTH = GROUP * HEAD_DIM

epsilon = 1e-06
theta = 1000000.0
scale = HEAD_DIM ** (-0.5)

BF = jnp.bfloat16
F32 = jnp.float32
CHIPS = ("cz", "cy")
VMEM = 56 * 1024 * 1024
SWAP = [(0, 1), (1, 0)]
NT = (((1,), (1,)), ((), ()))
TN = (((0,), (0,)), ((), ()))


def swap(values, axis):
    return lax.ppermute(values, axis, SWAP)


def dot(left, right, dims=(((1,), (0,)), ((), ()))):
    return lax.dot_general(left, right, dims, preferred_element_type=F32)


def rms_scale(rows, gain):
    inverse = lax.rsqrt(jnp.mean(rows * rows, axis=-1, keepdims=True) + epsilon)
    return rows * inverse * gain


def project_kernel(x_ref, gain_ref, w_ref, b_ref, cos_ref, sin_ref, first_ref, q_ref, kv_ref):
    rows = x_ref[...].astype(F32)
    first = rms_scale(rows, gain_ref[...]).astype(BF)
    first_ref[...] = first
    pre = dot(first, w_ref[...]) + b_ref[...]
    turned = Q_WIDTH + HEAD_DIM
    cosine = jnp.concatenate([cos_ref[...]] * (turned // 128), axis=1)
    sine = jnp.concatenate([sin_ref[...]] * (turned // 128), axis=1)
    front = pre[:, :turned]
    lane = lax.broadcasted_iota(jnp.int32, front.shape, 1) % HEAD_DIM
    other = jnp.where(
        lane < HALF, pltpu.roll(front, turned - HALF, 1), pltpu.roll(front, HALF, 1)
    )
    rot = front * cosine + other * sine
    q_ref[...] = (rot[:, :Q_WIDTH] * scale).astype(BF)
    kv_ref[...] = jnp.concatenate([rot[:, Q_WIDTH:], pre[:, turned:]], axis=1).astype(BF)


def project(rows, gain, weight, bias, cosine, sine):
    count, width = rows.shape
    wide = weight.shape[1]
    step = 256
    row_block = lambda n: pl.BlockSpec((step, n), lambda i: (i, 0))
    whole = lambda a, b: pl.BlockSpec((a, b), lambda i: (0, 0))
    return pl.pallas_call(
        project_kernel,
        grid=(count // step,),
        in_specs=[
            row_block(width),
            whole(1, width),
            whole(width, wide),
            whole(1, wide),
            row_block(128),
            row_block(128),
        ],
        out_specs=[row_block(width), row_block(Q_WIDTH), row_block(2 * HEAD_DIM)],
        out_shape=[
            jax.ShapeDtypeStruct((count, width), BF),
            jax.ShapeDtypeStruct((count, Q_WIDTH), BF),
            jax.ShapeDtypeStruct((count, 2 * HEAD_DIM), BF),
        ],
        compiler_params=pltpu.CompilerParams(vmem_limit_bytes=VMEM),
        cost_estimate=pl.CostEstimate(
            flops=2 * count * width * wide, bytes_accessed=count * width * 4, transcendentals=0
        ),
    )(rows, gain, weight, bias, cosine, sine)


def stack_heads(flat):
    return jnp.concatenate(
        [flat[:, h * HEAD_DIM : (h + 1) * HEAD_DIM] for h in range(GROUP)], axis=0
    )


def run_order(starts_ref, seq, index):
    one, two = starts_ref[seq, 2 * index], starts_ref[seq, 2 * index + 1]
    late = jnp.where(one > two, BLK, 0)
    low = pl.multiple_of(late, BLK)
    high = pl.multiple_of(BLK - late, BLK)
    return low, high, jnp.minimum(one, two), jnp.maximum(one, two)


def load_rows(own_ref, seq, ref):
    lows, highs = [], []
    for i in range(2):
        low, high, _, _ = run_order(own_ref, seq, i)
        lows.append(ref[i, 0, pl.ds(low, BLK), :])
        highs.append(ref[i, 0, pl.ds(high, BLK), :])
    return [stack_heads(jnp.concatenate(rows, axis=0)) for rows in (lows, highs)]


def store_rows(own_ref, seq, ref, lows, highs):
    for i in range(2):
        low, high, _, _ = run_order(own_ref, seq, i)
        ref[i, 0, pl.ds(low, BLK), :] = lows[i * BLK : (i + 1) * BLK].astype(BF)
        ref[i, 0, pl.ds(high, BLK), :] = highs[i * BLK : (i + 1) * BLK].astype(BF)


def load_keys(starts_ref, own_ref, seq, kv_ref, keys_ref, low_ref, high_ref):
    half = keys_ref.shape[0] // 2
    wide = low_ref.shape[1]
    lane = lax.broadcasted_iota(jnp.int32, (1, wide), 1) % (2 * BLK)
    inside = lax.broadcasted_iota(jnp.int32, (BLK, wide), 0)
    _, _, low_a, high_a = run_order(own_ref, seq, 0)
    _, _, low_b, high_b = run_order(own_ref, seq, 1)
    low_pos = jnp.where(lane < BLK, low_a, low_b) + lane % BLK
    high_pos = jnp.where(lane < BLK, high_a, high_b) + lane % BLK
    for r in range(half // BLK):
        low, high, low_start, high_start = run_order(starts_ref, seq, r)
        at = r * BLK
        keys_ref[at : at + BLK, :] = kv_ref[r // 2, r % 2, 0, pl.ds(low, BLK), :]
        keys_ref[half + at : half + at + BLK, :] = kv_ref[r // 2, r % 2, 0, pl.ds(high, BLK), :]
        low_ref[at : at + BLK, :] = jnp.where(inside + low_start <= low_pos, 0.0, -1e30)
        high_ref[at : at + BLK, :] = jnp.where(inside + high_start <= high_pos, 0.0, -1e30)


def query_chunks():
    total = GROUP * 2 * BLK
    return [(lo, min(lo + 256, total)) for lo in range(0, total, 256)]


def head_slices(values):
    return [values[:, at : at + 2 * BLK] for at in range(0, values.shape[1], 2 * BLK)]


def attend_kernel(
    offset, starts_ref, own_ref, q_ref, kv_ref, o_ref, lse_ref, keys_ref, low_ref, high_ref
):
    seq = pl.program_id(0) + offset
    half = keys_ref.shape[0] // 2
    load_keys(starts_ref, own_ref, seq, kv_ref, keys_ref, low_ref, high_ref)
    kv = keys_ref[...]
    key_low, key_high = kv[:half, :HEAD_DIM], kv[half:, :HEAD_DIM]
    value_t = kv.astype(F32).T[HEAD_DIM:].astype(BF)
    value_low, value_high = value_t[:, :half], value_t[:, half:]
    query_low, query_high = load_rows(own_ref, seq, q_ref)
    lows, highs = [], []
    for lo, hi in query_chunks():
        scores = dot(key_low, query_low[lo:hi], NT) + low_ref[:, : hi - lo]
        top = jnp.max(scores, axis=0, keepdims=True)
        expo = jnp.exp(scores - top)
        total = jnp.sum(expo, axis=0, keepdims=True)
        out = dot(value_low, expo.astype(BF)) / total
        lse_ref[0, 0:1, lo:hi] = top + jnp.log(total)
        lows += [part.T for part in head_slices(out)]
        first = dot(key_low, query_high[lo:hi], NT)
        second = dot(key_high, query_high[lo:hi], NT) + high_ref[:, : hi - lo]
        top = jnp.maximum(
            jnp.max(first, axis=0, keepdims=True), jnp.max(second, axis=0, keepdims=True)
        )
        first, second = jnp.exp(first - top), jnp.exp(second - top)
        total = jnp.sum(first, axis=0, keepdims=True) + jnp.sum(second, axis=0, keepdims=True)
        out = (dot(value_low, first.astype(BF)) + dot(value_high, second.astype(BF))) / total
        lse_ref[0, 1:2, lo:hi] = top + jnp.log(total)
        highs += [part.T for part in head_slices(out)]
    store_rows(
        own_ref, seq, o_ref, jnp.concatenate(lows, axis=1), jnp.concatenate(highs, axis=1)
    )


def attend_back_kernel(
    offset,
    starts_ref,
    own_ref,
    q_ref,
    kv_ref,
    do_ref,
    lse_ref,
    cos_ref,
    sin_ref,
    dq_ref,
    dkv_ref,
    keys_ref,
    low_ref,
    high_ref,
    probs_ref,
    grads_ref,
):
    seq = pl.program_id(0) + offset
    half = keys_ref.shape[0] // 2
    wide = probs_ref.shape[1] // 2
    total = GROUP * 2 * BLK
    load_keys(starts_ref, own_ref, seq, kv_ref, keys_ref, low_ref, high_ref)
    kv = keys_ref[...]
    key_low, key_high = kv[:half, :HEAD_DIM], kv[half:, :HEAD_DIM]
    value_low, value_high = kv[:half, HEAD_DIM:], kv[half:, HEAD_DIM:]
    key_t = kv.astype(F32).T[:HEAD_DIM].astype(BF)
    query_low, query_high = load_rows(own_ref, seq, q_ref)
    out_low, out_high = load_rows(own_ref, seq, do_ref)

    def tables(ref):
        table = ref[0]
        lows, highs = [], []
        for i in range(2):
            one, two = own_ref[seq, 2 * i], own_ref[seq, 2 * i + 1]
            front = table[:, 2 * i * BLK : (2 * i + 1) * BLK]
            back = table[:, (2 * i + 1) * BLK : (2 * i + 2) * BLK]
            lows.append(jnp.where(one > two, back, front))
            highs.append(jnp.where(one > two, front, back))
        return jnp.concatenate(lows, axis=1), jnp.concatenate(highs, axis=1)

    cos_low, cos_high = tables(cos_ref)
    sin_low, sin_high = tables(sin_ref)

    def unturned(grad_q, cosine, sine):
        heads = []
        for part in head_slices(grad_q):
            front, back = part[:HALF], part[HALF:]
            heads.append(
                jnp.concatenate(
                    [front * cosine + back * sine, back * cosine - front * sine], axis=0
                ).T
            )
        return heads

    lows, highs = [], []
    for lo, hi in query_chunks():
        scores = dot(key_low, query_low[lo:hi], NT) + low_ref[:, : hi - lo]
        probs = jnp.exp(scores - lse_ref[0, 0:1, lo:hi])
        probs_ref[:half, lo:hi] = probs.astype(BF)
        grad_p = dot(value_low, out_low[lo:hi], NT)
        inner = jnp.sum(probs * grad_p, axis=0, keepdims=True)
        grad_s = (probs * (grad_p - inner)).astype(BF)
        grads_ref[:half, lo:hi] = grad_s
        lows += unturned(dot(key_t[:, :half], grad_s) * scale, cos_low, sin_low)
        lse = lse_ref[0, 1:2, lo:hi]
        at, to = wide + lo, wide + hi
        first = jnp.exp(dot(key_low, query_high[lo:hi], NT) - lse)
        second = jnp.exp(dot(key_high, query_high[lo:hi], NT) + high_ref[:, : hi - lo] - lse)
        probs_ref[:half, at:to] = first.astype(BF)
        probs_ref[half:, at:to] = second.astype(BF)
        grad_first = dot(value_low, out_high[lo:hi], NT)
        grad_second = dot(value_high, out_high[lo:hi], NT)
        inner = jnp.sum(first * grad_first, axis=0, keepdims=True) + jnp.sum(
            second * grad_second, axis=0, keepdims=True
        )
        grad_first = (first * (grad_first - inner)).astype(BF)
        grad_second = (second * (grad_second - inner)).astype(BF)
        grads_ref[:half, at:to] = grad_first
        grads_ref[half:, at:to] = grad_second
        grad_q = dot(key_t[:, :half], grad_first) + dot(key_t[:, half:], grad_second)
        highs += unturned(grad_q * scale, cos_high, sin_high)
    store_rows(
        own_ref, seq, dq_ref, jnp.concatenate(lows, axis=1), jnp.concatenate(highs, axis=1)
    )

    def key_grads(ref, left, right):
        low = dot(ref[:half, :total], left) + dot(ref[:half, wide : wide + total], right)
        return low, dot(ref[half:, wide : wide + total], right)

    key_parts = key_grads(grads_ref, query_low, query_high)
    value_parts = key_grads(probs_ref, out_low, out_high)
    grad_low, grad_high = [
        jnp.concatenate([key, value], axis=1).astype(BF)
        for key, value in zip(key_parts, value_parts)
    ]
    for r in range(half // BLK):
        low, high, _, _ = run_order(starts_ref, seq, r)
        at = r * BLK
        dkv_ref[r // 2, r % 2, 0, pl.ds(low, BLK), :] = grad_low[at : at + BLK]
        dkv_ref[r // 2, r % 2, 0, pl.ds(high, BLK), :] = grad_high[at : at + BLK]


def attention(back, offset, seqs, starts, own, q, kv, *more):
    run = q.shape[2]
    assert run == 2 * BLK
    chips = kv.shape[0]
    local = 2 * run
    keys = chips * local
    total = GROUP * local
    wide = 512
    q_spec = pl.BlockSpec((2, 1, run, Q_WIDTH), lambda s, st, ow: (0, s + offset, 0, 0))
    part_spec = pl.BlockSpec((2, 1, run, Q_WIDTH), lambda s, st, ow: (0, s, 0, 0))
    kv_block = (chips, 2, 1, run, 2 * HEAD_DIM)
    kv_spec = pl.BlockSpec(kv_block, lambda s, st, ow: (0, 0, s + offset, 0, 0))
    kv_part_spec = pl.BlockSpec(kv_block, lambda s, st, ow: (0, 0, s, 0, 0))
    lse_spec = pl.BlockSpec((1, 2, wide), lambda s, st, ow: (s + offset, 0, 0))
    turn_spec = pl.BlockSpec((1, HALF, local), lambda s, st, ow: (s + offset, 0, 0))
    in_specs = [q_spec, kv_spec]
    scratch = [
        pltpu.VMEM((keys, 2 * HEAD_DIM), BF),
        pltpu.VMEM((keys // 2, 256), F32),
        pltpu.VMEM((keys // 2, 256), F32),
    ]
    part_shape = jax.ShapeDtypeStruct((2, seqs, run, Q_WIDTH), BF)
    if back:
        in_specs += [q_spec, lse_spec, turn_spec, turn_spec]
        out_specs = [part_spec, kv_part_spec]
        kv_shape = kv.shape[:2] + (seqs,) + kv.shape[3:]
        out_shape = [part_shape, jax.ShapeDtypeStruct(kv_shape, BF)]
        scratch += [pltpu.VMEM((keys, 2 * wide), BF)] * 2
    else:
        out_specs = [part_spec, lse_spec]
        out_shape = [part_shape, jax.ShapeDtypeStruct((seqs, 2, wide), F32)]
    passes = 5 if back else 2
    return pl.pallas_call(
        functools.partial(attend_back_kernel if back else attend_kernel, offset),
        grid_spec=pltpu.PrefetchScalarGridSpec(
            num_scalar_prefetch=2,
            grid=(seqs,),
            in_specs=in_specs,
            out_specs=out_specs,
            scratch_shapes=scratch,
        ),
        out_shape=out_shape,
        compiler_params=pltpu.CompilerParams(vmem_limit_bytes=VMEM),
        cost_estimate=pl.CostEstimate(
            flops=8 * passes * seqs * keys * total * HEAD_DIM,
            bytes_accessed=seqs * keys * 512,
            transcendentals=seqs * keys * total,
        ),
    )(starts, own, q, kv, *more)


def mlp_kernel(s_ref, c_ref, g_ref, u_ref, d_ref, hid_ref, gg_ref, gu_ref, mix_ref, gs_ref):
    rows = s_ref[...]
    grad = c_ref[...]
    wide = g_ref.shape[1]
    for lo in range(0, wide, 256):
        hi = min(lo + 256, wide)
        gate = dot(rows, g_ref[:, lo:hi])
        up = dot(rows, u_ref[:, lo:hi])
        grad_hidden = dot(grad, d_ref[lo:hi, :], NT)
        sig = 1.0 / (1.0 + jnp.exp(-gate))
        silu = gate * sig
        hid_ref[:, lo:hi] = (silu * up).astype(BF)
        gg_ref[:, lo:hi] = (grad_hidden * up * (sig * (1.0 + gate * (1.0 - sig)))).astype(BF)
        gu_ref[:, lo:hi] = (grad_hidden * silu).astype(BF)
    mix_ref[...] = dot(hid_ref[...], d_ref[...]).astype(BF)
    gs_ref[...] = (dot(gg_ref[...], g_ref[...], NT) + dot(gu_ref[...], u_ref[...], NT)).astype(BF)


def mlp(rows, grad, gate_w, up_w, down_w):
    count, width = rows.shape
    wide = gate_w.shape[1]
    step = 256
    row_block = lambda n: pl.BlockSpec((step, n), lambda i: (i, 0))
    whole = lambda a, b: pl.BlockSpec((a, b), lambda i: (0, 0))
    shape = lambda n: jax.ShapeDtypeStruct((count, n), BF)
    return pl.pallas_call(
        mlp_kernel,
        grid=(count // step,),
        in_specs=[
            row_block(width),
            row_block(width),
            whole(width, wide),
            whole(width, wide),
            whole(wide, width),
        ],
        out_specs=[row_block(wide)] * 3 + [row_block(width)] * 2,
        out_shape=[shape(wide)] * 3 + [shape(width)] * 2,
        compiler_params=pltpu.CompilerParams(vmem_limit_bytes=VMEM),
        cost_estimate=pl.CostEstimate(
            flops=12 * count * width * wide,
            bytes_accessed=count * (wide * 6 + width * 8),
            transcendentals=count * wide,
        ),
    )(rows, grad, gate_w, up_w, down_w)


def weight_grad_kernel(pair_ref, a_near, a_far, b_near, b_far, keep_ref, send_ref, acc_ref):
    step = pl.program_id(0)
    steps = pl.num_programs(0)

    @pl.when(step == 0)
    def _():
        acc_ref[...] = dot(a_near[...], b_near[...], TN)

    @pl.when(jnp.logical_and(step > 0, step < steps // 2))
    def _():
        acc_ref[...] += dot(a_near[...], b_near[...], TN)

    @pl.when(step >= steps // 2)
    def _():
        acc_ref[...] += dot(a_far[...], b_far[...], TN)

    @pl.when(step == steps - 1)
    def _():
        outer, parts, tall, _ = keep_ref.shape
        tiles = acc_ref.shape[1] // 128
        high = tall // tiles
        slab = parts * high
        for out_ref, which in ((keep_ref, pair_ref[0]), (send_ref, 1 - pair_ref[0])):
            for o in range(outer):
                start = pl.multiple_of((2 * o + which) * slab, slab)
                for t in range(tiles):
                    tile = acc_ref[pl.ds(start, slab), t * 128 : (t + 1) * 128].astype(BF)
                    for z in range(parts):
                        out_ref[o, z, t * high : (t + 1) * high, :] = tile[
                            z * high : (z + 1) * high
                        ]


def weight_grad(pair, outer, parts, near, far):
    (a_near, b_near), (a_far, b_far) = near, far
    count, high = a_near.shape
    wide = b_near.shape[1]
    half = 2
    step = count // half
    tall = high // (2 * outer * parts) * (wide // 128)
    near_block = lambda n: pl.BlockSpec((step, n), lambda i, p: (jnp.minimum(i, half - 1), 0))
    far_block = lambda n: pl.BlockSpec((step, n), lambda i, p: (jnp.maximum(i - half, 0), 0))
    out_spec = pl.BlockSpec((outer, parts, tall, 128), lambda i, p: (0, 0, 0, 0))
    shape = jax.ShapeDtypeStruct((outer, parts, tall, 128), BF)
    return pl.pallas_call(
        weight_grad_kernel,
        grid_spec=pltpu.PrefetchScalarGridSpec(
            num_scalar_prefetch=1,
            grid=(2 * half,),
            in_specs=[near_block(high), far_block(high), near_block(wide), far_block(wide)],
            out_specs=[out_spec, out_spec],
            scratch_shapes=[pltpu.VMEM((high, wide), F32)],
        ),
        out_shape=[shape, shape],
        compiler_params=pltpu.CompilerParams(vmem_limit_bytes=VMEM),
        cost_estimate=pl.CostEstimate(
            flops=4 * count * high * wide,
            bytes_accessed=4 * count * (high + wide),
            transcendentals=0,
        ),
    )(pair, a_near, a_far, b_near, b_far)


def spread_rows_kernel(skip, in_ref, out_ref):
    parts, windows, _, tall, _ = in_ref.shape
    tiles = out_ref.shape[1] // 128
    high = tall // tiles
    for q in range(windows):
        drop = skip if q == windows - 1 else 0
        for z in range(parts):
            lo = max(drop - z * high, 0)
            if lo >= high:
                continue
            at = q * parts * high + z * high + lo - drop
            for t in range(tiles):
                out_ref[at : at + high - lo, t * 128 : (t + 1) * 128] = in_ref[
                    z, q, 0, t * high + lo : (t + 1) * high, :
                ].astype(F32)


def spread_rows(every, skip, part):
    parts, windows, _, tall, _ = every.shape
    width = tall * parts * 128 // ((part + skip) // windows)
    return pl.pallas_call(
        functools.partial(spread_rows_kernel, skip),
        grid=(1,),
        in_specs=[pl.BlockSpec((parts, windows, 1, tall, 128), lambda i: (0, 0, 0, 0, 0))],
        out_specs=pl.BlockSpec((part, width), lambda i: (0, 0)),
        out_shape=jax.ShapeDtypeStruct((part, width), F32),
        compiler_params=pltpu.CompilerParams(vmem_limit_bytes=VMEM),
    )(every)


def spread_columns_kernel(owners, part, begins, skips, gate_ref, up_ref, gate_out, up_out):
    high = gate_out.shape[0]
    tiles = gate_ref.shape[3] // high // owners
    for in_ref, out_ref in ((gate_ref, gate_out), (up_ref, up_out)):
        for owner in range(owners):
            for q in range(4):
                for t in range(skips[q] // 128, tiles):
                    at = owner * part + begins[q] + 128 * t
                    row = (owner * tiles + t) * high
                    out_ref[:, at : at + 128] = in_ref[0, q, 0, row : row + high, :].astype(F32)


def spread_columns(every, owners, part, begins, skips):
    parts, _, _, tall, _ = every.shape
    window = part - begins[3]
    high = tall * 128 // (owners * window)
    block = (1, 4, 1, tall, 128)
    out_spec = pl.BlockSpec((high, owners * part), lambda z: (z, 0))
    shape = jax.ShapeDtypeStruct((parts * high, owners * part), F32)
    return pl.pallas_call(
        functools.partial(spread_columns_kernel, owners, part, begins, skips),
        grid=(parts,),
        in_specs=[
            pl.BlockSpec(block, lambda z: (z, 0, 1, 0, 0)),
            pl.BlockSpec(block, lambda z: (z, 0, 2, 0, 0)),
        ],
        out_specs=[out_spec, out_spec],
        out_shape=[shape, shape],
        compiler_params=pltpu.CompilerParams(vmem_limit_bytes=VMEM),
    )(every, every)


def gather_small(values, axis, size):
    out = values[None]
    index = lax.axis_index(axis)
    bit = 1
    while bit < size:
        other = lax.ppermute(out, axis, [(i, i ^ bit) for i in range(size)])
        low = (index & bit) == 0
        out = jnp.where(
            low, jnp.concatenate([out, other], axis=0), jnp.concatenate([other, out], axis=0)
        )
        bit *= 2
    return out


def line_part(values, at):
    at = jnp.clip(at, 0, values.shape[0] - 1)
    return lax.dynamic_index_in_dim(values, at, 0, keepdims=False).astype(F32)


def line_load(values, axis, step, arrived):
    size = values.shape[0]
    index = lax.axis_index(axis)
    far = size - 1 - step
    up, down = line_part(values, index + far), line_part(values, index - far)
    if step:
        up, down = up + arrived[0].astype(F32), down + arrived[1].astype(F32)
    return up.astype(BF), down.astype(BF)


def line_send(load, axis, size, step):
    far = size - 1 - step
    right = [(i, i + 1) for i in range(size - 1) if i <= step]
    left = [(i + 1, i) for i in range(size - 1) if i + 1 >= far]
    return lax.ppermute(load[0], axis, right), lax.ppermute(load[1], axis, left)


def line_total(values, axis, arrived):
    own = line_part(values, lax.axis_index(axis))
    return (own + arrived[0].astype(F32) + arrived[1].astype(F32)).astype(BF)


def line_gather(values, axis, size):
    index = lax.axis_index(axis)
    right = left = values
    rights, lefts = [], []
    for step in range(size - 1):
        right = lax.ppermute(right, axis, [(i, i + 1) for i in range(size - 1) if i >= step])
        left = lax.ppermute(
            left, axis, [(i + 1, i) for i in range(size - 1) if i + 1 <= size - 1 - step]
        )
        rights.append(right)
        lefts.append(left)
    row = jnp.stack(rights[::-1] + [values] + lefts)
    return lax.dynamic_slice_in_dim(row, size - 1 - index, size, 0)


def pair_sum(values, axis, size):
    bit = 1
    while bit < size:
        other = lax.ppermute(values, axis, [(i, i ^ bit) for i in range(size)])
        values = (values.astype(F32) + other.astype(F32)).astype(values.dtype)
        bit *= 2
    return values


def together(*values):
    return lax.optimization_barrier(values)


def make_body(sizes):
    cz, outer = sizes["cz"], sizes["outer"]
    chips = cz * sizes["cy"]
    owners = 2 * outer

    def ordered(axis, own, other):
        low = lax.axis_index(axis) == 0
        return jnp.where(low, own, other), jnp.where(low, other, own)

    def gather_rows(values):
        rows = values.shape[0]
        if outer > 1:
            values = lax.all_gather(values, "outer", axis=0)
        else:
            values = values[None]
        both = jnp.stack(ordered("pair", values, swap(values, "pair")), axis=1)
        return both.reshape((owners * rows,) + values.shape[2:])

    def gather_start(values):
        if outer > 1:
            values = lax.all_gather(values, "outer", axis=0)
        else:
            values = values[None]
        return swap(values, "pair")

    def gather_finish(values, far):
        if outer > 1:
            values = lax.all_gather(values, "outer", axis=0)
        else:
            values = values[None]
        both = jnp.stack(ordered("pair", values, far), axis=1)
        return both.reshape((owners * values.shape[1],) + values.shape[2:])

    def gather_chips(values):
        return lax.all_gather(values, CHIPS, axis=0)

    def split_cy(values, axis):
        half = values.shape[axis] // 2
        first = lax.slice_in_dim(values, 0, half, axis=axis)
        last = lax.slice_in_dim(values, half, 2 * half, axis=axis)
        low = lax.axis_index("cy") == 0
        return jnp.where(low, first, last), jnp.where(low, last, first)

    def split_owners(values):
        split = values.reshape(outer, 2, -1, values.shape[1])
        if outer > 1:
            split = lax.psum_scatter(split, "outer", scatter_dimension=0)
        else:
            split = split[0]
        low = lax.axis_index("pair") == 0
        return jnp.where(low, split[0], split[1]), jnp.where(low, split[1], split[0])

    def add(left, right):
        return (left.astype(F32) + right.astype(F32)).astype(left.dtype)

    def bits_of(size):
        return [1 << b for b in range((size - 1).bit_length())]

    def exchange(values, axis, size, bit):
        return lax.ppermute(values, axis, [(i, i ^ bit) for i in range(size)])

    def body(
        tokens,
        positions,
        cotangent,
        query_weight,
        key_weight,
        value_weight,
        out_weight,
        gate_weight,
        up_weight,
        down_weight,
        query_bias,
        key_bias,
        value_bias,
        first_gain,
        second_gain,
    ):
        core0 = lax.axis_index("core") == 0
        pair = lax.axis_index("pair")
        quarter = 2 * lax.axis_index("cy") + lax.axis_index("core")
        seqs, run, width = tokens.shape
        rows = seqs * run
        ff = gate_weight.shape[1]
        part = down_weight.shape[0]
        window = min(part, -(-part // 512) * 128)
        begins = [min(q * window, part - window) for q in range(4)]
        skips = [min(q * window - begins[q], window) for q in range(4)]
        slab = gate_weight.shape[0]

        def heads_of(values, each):
            return jnp.where(core0, values[..., :each], values[..., each:])

        places = jnp.stack([positions, swap(positions, "core")])
        firsts = places[:, :, ::BLK]
        starts = gather_small(gather_small(firsts, "cy", 2), "cz", cz)
        starts = starts.transpose(3, 0, 1, 2, 4).reshape(seqs, -1)
        own_starts = firsts.transpose(1, 0, 2).reshape(seqs, 4)
        turned = Q_WIDTH + HEAD_DIM
        kv_rows = key_bias.shape[0]
        vectors = jnp.concatenate([query_bias, key_bias, value_bias, first_gain, second_gain])
        lanes = vectors.shape[0]
        wide = turned + HEAD_DIM
        lines = -(-lanes // wide)
        vectors = jnp.concatenate([vectors, jnp.zeros((16 * wide - lanes,), BF)]).reshape(16, wide)
        qkv_local = jnp.concatenate(
            [
                jnp.concatenate(
                    [
                        heads_of(query_weight, Q_WIDTH),
                        heads_of(key_weight, HEAD_DIM),
                        heads_of(value_weight, HEAD_DIM),
                    ],
                    axis=1,
                ),
                vectors,
            ]
        )
        tokens_far = swap(tokens, "core")
        def by_quarter(choices):
            out = choices[3]
            for q in range(3):
                out = jnp.where(quarter == q, choices[q], out)
            return out

        def columns(values, q):
            at = [owner * part + begins[q] for owner in range(owners)]
            return jnp.concatenate([values[:, a : a + window] for a in at], axis=1)

        inside = lax.broadcasted_iota(jnp.int32, (1, owners * window), 1) % window
        skip = by_quarter([jnp.int32(n) for n in skips])

        def units(values):
            full = by_quarter([columns(values, q) for q in range(4)])
            return jnp.where(inside < skip, jnp.zeros((), BF), full)

        gate_own = units(gate_weight)
        up_own = units(up_weight)
        down_own = by_quarter([down_weight[at : at + window] for at in begins])
        qkv_all = gather_rows(qkv_local)
        qkv_all, gate_own, up_own, out_own, down_own, starts, own_starts = lax.optimization_barrier(
            (qkv_all, gate_own, up_own, out_weight, down_own, starts, own_starts)
        )
        qkv_all = qkv_all.reshape(owners, slab + 16, wide)
        qkv = qkv_all[:, :slab].reshape(owners * slab, wide)
        vectors = qkv_all[:, slab:].reshape(owners, -1)

        def vector_of(at, size):
            return vectors[:, at : at + size].reshape(-1)

        qb = vector_of(0, slab)
        kb = vector_of(slab, kv_rows)
        vb = vector_of(slab + kv_rows, kv_rows)
        fgain = vector_of(slab + 2 * kv_rows, slab).astype(F32)
        sgain = vector_of(2 * slab + 2 * kv_rows, slab).astype(F32)
        bias = jnp.concatenate(
            [heads_of(qb, Q_WIDTH), heads_of(kb, HEAD_DIM), heads_of(vb, HEAD_DIM)]
        ).astype(F32)[None]
        if outer > 1:
            out_full = gather_rows(out_own)
            out_w = jnp.where(core0, out_full[:Q_WIDTH], out_full[Q_WIDTH:])
        else:
            out_far = lax.ppermute(out_own, ("core", "pair"), [(0, 1), (3, 2)])
            out_w = jnp.where(lax.axis_index("core") == pair, out_own, out_far)
        down_w = gather_rows(down_own)

        freq = theta ** (-jnp.arange(HALF, dtype=F32) / HALF)
        angles = places.reshape(2 * rows, 1).astype(F32) * freq
        cosine, sine = jnp.cos(angles), jnp.sin(angles)
        cos_wide = jnp.concatenate([cosine] * 4, axis=1)
        sin_wide = jnp.concatenate([-sine, sine] * 2, axis=1)

        def turned_rows(table):
            table = table.reshape(2, seqs, run, HALF).transpose(1, 3, 0, 2)
            return table.reshape(seqs, HALF, 2 * run)

        own_rows = tokens.reshape(rows, width)
        chip_rows = jnp.concatenate([own_rows, tokens_far.reshape(rows, width)])
        first, q, kv = project(
            chip_rows, fgain[None], qkv, bias, cos_wide, sin_wide
        )
        q = q.reshape(2, seqs, run, Q_WIDTH)
        kv = kv.reshape(2, seqs, run, 2 * HEAD_DIM)
        cut = seqs // 2
        kv_all = gather_chips(kv)
        gate_far = gather_start(gate_own)
        kv_all, out_w, down_w, gate_far, cot_late, up_own = together(
            kv_all, out_w, down_w, gate_far, cotangent, up_own
        )
        up_far = gather_start(up_own)
        grad_own = cot_late.reshape(rows, width)
        far_grad = swap(grad_own, "cy")
        attn, lse = attention(False, 0, seqs, starts, own_starts, q, kv_all)
        attn_rows = attn.reshape(2 * rows, Q_WIDTH)
        attn_rows, up_far, far_grad = together(attn_rows, up_far, far_grad)
        gate_w = gather_finish(gate_own, gate_far)
        up_w = gather_finish(up_own, up_far)
        attn_part = dot(attn_rows, out_w).astype(BF)
        inputs = own_rows.astype(F32)
        middle = (
            inputs
            + attn_part[:rows].astype(F32)
            + swap(attn_part[rows:], "core").astype(F32)
        )

        second = rms_scale(middle, sgain).astype(BF)
        near_c = jnp.concatenate([grad_own, swap(grad_own, "core")])
        far_c = jnp.concatenate([far_grad, swap(far_grad, "core")])
        far_second = swap(second, "cy")
        near_s = jnp.concatenate([second, swap(second, "core")])
        near_h, near_g, near_u, near_mix, near_gs = mlp(near_s, near_c, gate_w, up_w, down_w)
        far_second, near_h, near_g, near_u, near_mix, near_gs = together(
            far_second, near_h, near_g, near_u, near_mix, near_gs
        )
        far_core, gs_core = together(swap(far_second, "core"), swap(near_gs[rows:], "core"))
        far_s = jnp.concatenate([far_second, far_core])
        far_h, far_g, far_u, far_mix, far_gs = mlp(far_s, far_c, gate_w, up_w, down_w)
        own_gs = near_gs[:rows].astype(F32) + gs_core.astype(F32)
        send_gs = add(far_gs[:rows], swap(far_gs[rows:], "core"))

        send_gs, far_h, far_g, far_u, far_mix = together(send_gs, far_h, far_g, far_u, far_mix)
        back_gs = swap(send_gs, "cy")
        pair_index = jnp.reshape(pair, (1,)).astype(jnp.int32)

        def unit_grad(near, far):
            keep, send = weight_grad(pair_index, outer, cz, near, far)
            if outer > 1:
                keep = lax.psum_scatter(keep, "outer", scatter_dimension=0)
                send = lax.psum_scatter(send, "outer", scatter_dimension=0)
                return keep, send
            return keep[0], send[0]

        keep_down, send_down = unit_grad((near_h, near_c), (far_h, far_c))
        keep_down, send_down, far_g, near_mix, far_mix = together(
            keep_down, send_down, far_g, near_mix, far_mix
        )
        sum_down = swap(send_down, "pair")
        mix_near_core = swap(near_mix[rows:], "core")
        mix_far_core = swap(far_mix[rows:], "core")
        keep_gate, send_gate = unit_grad((near_s, near_g), (far_s, far_g))
        keep_gate, far_u = together(keep_gate, far_u)
        keep_up, send_up = unit_grad((near_s, near_u), (far_s, far_u))
        keep_up, back_gs, sum_down, mix_near_core, mix_far_core, send_gate, send_up = together(
            keep_up, back_gs, sum_down, mix_near_core, mix_far_core, send_gate, send_up
        )
        sum_gate, sum_up = swap(send_gate, "pair"), swap(send_up, "pair")
        send_mix = add(far_mix[:rows], mix_far_core)
        back_mix = swap(send_mix, "cy")
        grad_second = own_gs + back_gs.astype(F32)
        _, pull_second = jax.vjp(rms_scale, middle, sgain)
        grad_middle_part, grad_sgain = pull_second(grad_second)
        grad_middle = grad_own.astype(F32) + grad_middle_part
        grad_branch = grad_middle.astype(BF)
        grad_branch = jnp.concatenate([grad_branch, swap(grad_branch, "core")])
        grad_attn = dot(grad_branch, out_w, NT).astype(BF).reshape(2, seqs, run, Q_WIDTH)
        grad_out_w = dot(attn_rows, grad_branch, TN).astype(BF)
        cos_t, sin_t = turned_rows(cosine), turned_rows(sine)

        def attend_back(at, count, grad):
            return attention(True, at, count, starts, own_starts, q, kv_all, grad, lse, cos_t, sin_t)

        def keys_cy(values):
            return split_cy(values.reshape((cz, 2) + values.shape[1:]), 1)

        grad_q_near, grad_kv_near = attend_back(0, cut, grad_attn)
        grad_q_near, grad_kv_near, back_mix, sum_down, sum_gate, sum_up = together(
            grad_q_near, grad_kv_near, back_mix, sum_down, sum_gate, sum_up
        )
        mix_own = near_mix[:rows].astype(F32) + mix_near_core.astype(F32)
        mixed = (middle + mix_own + back_mix.astype(F32)).astype(BF).reshape(seqs, run, width)
        line = jnp.concatenate(
            [add(keep_down, sum_down), add(keep_gate, sum_gate), add(keep_up, sum_up)], axis=1
        )
        if outer > 1:
            every_out = jnp.concatenate(ordered("core", grad_out_w, swap(grad_out_w, "core")))
            keep_out, send_out = split_owners(every_out)
            out_rows = add(keep_out, swap(send_out, "pair"))
        else:
            far_out = lax.ppermute(grad_out_w, ("core", "pair"), [(1, 0), (2, 3)])
            out_rows = add(grad_out_w, far_out)
            mine_here = lax.axis_index("core") == pair
            out_rows = jnp.where(mine_here, out_rows, swap(out_rows, "core"))
        out_rows = heads_of(out_rows, width // 2)

        keep_near, send_near = keys_cy(grad_kv_near)
        load = line_load(line, "cz", 0, None)
        keep_out, send_out = split_cy(out_rows, 0)
        load, send_near, grad_late, send_out = together(load, send_near, grad_attn, send_out)
        far_out = swap(send_out, "cy")
        arrived = line_send(load, "cz", cz, 0)
        back_near = swap(send_near, "cy")
        grad_q_far, grad_kv_far = attend_back(cut, seqs - cut, grad_late)
        grad_q_far, grad_kv_far, arrived, back_near, far_out = together(
            grad_q_far, grad_kv_far, arrived, back_near, far_out
        )
        out_sum = add(keep_out, far_out)
        grad_q = jnp.concatenate([grad_q_near, grad_q_far], axis=1).reshape(2 * rows, Q_WIDTH)
        grad_q_w = dot(first, grad_q, TN).astype(BF)
        keep_far, send_far = keys_cy(grad_kv_far)
        keep_early, send_early = split_owners(grad_q_w)
        bits = bits_of(cz)
        load = line_load(line, "cz", 1, arrived)
        load, send_far, out_sum = together(load, send_far, out_sum)
        arrived, back_far, far_out = together(
            line_send(load, "cz", cz, 1),
            swap(send_far, "cy"),
            exchange(out_sum, "cz", cz, bits[0]),
        )
        out_sum = add(out_sum, far_out)
        keys = [add(keep_near, back_near), add(keep_far, back_far)]
        keys = jnp.concatenate(keys, axis=3).reshape(cz, 2 * rows, 2 * HEAD_DIM)
        load, keys_load = line_load(line, "cz", 2, arrived), line_load(keys, "cz", 0, None)
        load, keys_load, send_early, out_sum = together(load, keys_load, send_early, out_sum)
        arrived, keys_arrived, far_early, far_out = together(
            line_send(load, "cz", cz, 2),
            line_send(keys_load, "cz", cz, 0),
            swap(send_early, "pair"),
            exchange(out_sum, "cz", cz, bits[1]),
        )
        out_sum = add(out_sum, far_out)
        for bit in bits[2:]:
            out_sum = add(out_sum, exchange(out_sum, "cz", cz, bit))
        for step in range(3, cz - 1):
            arrived = line_send(line_load(line, "cz", step, arrived), "cz", cz, step)
        mine = line_total(line, "cz", arrived)
        early = add(keep_early, far_early)
        keep_early, send_early = split_cy(early, 0)
        keys_load = line_load(keys, "cz", 1, keys_arrived)
        mine, keys_load, send_early, out_sum = together(mine, keys_load, send_early, out_sum)
        keys_arrived, far_early, far_out = together(
            line_send(keys_load, "cz", cz, 1), swap(send_early, "cy"), swap(out_sum, "cy")
        )
        out_sum = jnp.concatenate(ordered("cy", out_sum, far_out))
        early = add(keep_early, far_early)
        for step in range(2, cz - 1):
            load = line_load(keys, "cz", step, keys_arrived)
            if step == 2:
                load, early, out_sum = together(load, early, out_sum)
                keys_arrived, far_early, far_sum = together(
                    line_send(load, "cz", cz, step),
                    exchange(early, "cz", cz, bits[0]),
                    swap(out_sum, "core"),
                )
                early = add(early, far_early)
            else:
                keys_arrived = line_send(load, "cz", cz, step)
        grad_kv = line_total(keys, "cz", keys_arrived).astype(F32)
        front = grad_kv[:, :HALF]
        back = grad_kv[:, HALF:HEAD_DIM]
        grad_kv = jnp.concatenate(
            [front * cosine + back * sine, back * cosine - front * sine, grad_kv[:, HEAD_DIM:]],
            axis=1,
        ).astype(BF)
        grad_qkv = jnp.concatenate([grad_q, grad_kv], axis=1)
        grad_kv_w = dot(first, grad_kv, TN).astype(BF)
        grad_biases = jnp.sum(grad_qkv.astype(F32), axis=0)
        grad_first_part = dot(grad_qkv, qkv, NT).astype(BF)
        keep_kv, send_kv = split_owners(grad_kv_w)
        for bit in bits[2:]:
            early = add(early, exchange(early, "cz", cz, bit))
        send_first, send_kv = together(grad_first_part[rows:], send_kv)
        far_early = exchange(early, "cz", cz, bits[1])
        far_first, far_kv = together(swap(send_first, "core"), swap(send_kv, "pair"))
        total_kv = add(keep_kv, far_kv)
        grad_first = grad_first_part[:rows].astype(F32) + far_first.astype(F32)
        _, pull_first = jax.vjp(rms_scale, inputs, fgain)
        grad_input_part, grad_fgain = pull_first(grad_first)
        grad_tokens = (grad_middle + grad_input_part).reshape(seqs, run, width)

        zeros = jnp.zeros((), F32)

        def spread(values):
            return jnp.concatenate(
                [jnp.where(core0, values, zeros), jnp.where(core0, zeros, values)]
            )

        vector = jnp.concatenate(
            [
                spread(grad_biases[:Q_WIDTH]),
                spread(grad_biases[Q_WIDTH:turned]),
                spread(grad_biases[turned:]),
                grad_fgain,
                grad_sgain,
            ]
        )
        hops = [("cz", cz, bit) for bit in bits] + [("cy", 2, 1)]
        for count, hop in enumerate(hops):
            total_kv, vector = together(total_kv, vector)
            last = count == len(hops) - 1
            sends = [exchange(total_kv, *hop), exchange(vector, *hop)] + [far_early] * last
            arrivals = together(*sends)
            total_kv, vector = add(total_kv, arrivals[0]), vector + arrivals[1]
            if last:
                early = add(early, arrivals[2])
        total_kv, vector = together(total_kv, vector)
        far_kv, far_vector, far_early = together(
            swap(total_kv, "core"), swap(vector, "core"), swap(early, "cy")
        )
        early = jnp.concatenate(ordered("cy", early, far_early))
        far_early = swap(early, "core")
        vector = vector + far_vector
        vector = pair_sum(vector, "pair", 2)
        if outer > 1:
            vector = pair_sum(vector, "outer", outer)
        out_query = jnp.concatenate(
            ordered("core", early.astype(F32), far_early.astype(F32)), axis=1
        )
        out_out = jnp.concatenate(
            ordered("core", out_sum.astype(F32), far_sum.astype(F32)), axis=1
        )
        low_kv, high_kv = ordered("core", total_kv.astype(F32), far_kv.astype(F32))
        out_key = jnp.concatenate([low_kv[:, :HEAD_DIM], high_kv[:, :HEAD_DIM]], axis=1)
        out_value = jnp.concatenate([low_kv[:, HEAD_DIM:], high_kv[:, HEAD_DIM:]], axis=1)
        owner = 2 * lax.axis_index("outer") + pair
        vectors = []
        at = 0
        for size in (width, KV_HEADS * HEAD_DIM, KV_HEADS * HEAD_DIM, width, width):
            share = size // owners
            vectors.append(lax.dynamic_slice(vector, (at + owner * share,), (share,)))
            at += size

        every = lax.all_gather(mine, CHIPS + ("core",), axis=0)
        every = every.reshape((cz, 4, 3, -1, 128))
        if part % 128 == 0 and not any(skips[:3]):
            out_down = spread_rows(every, skips[3], part)
            out_gate, out_up = spread_columns(every, owners, part, begins, skips)
        else:

            def windows(index, q, high):
                tiles = every[:, q, index].reshape(cz, -1, high // cz, 128)
                return tiles.transpose(0, 2, 1, 3).reshape(high, -1).astype(F32)

            out_down = jnp.concatenate(
                [windows(0, q, window)[skips[q] :] for q in range(4)]
            )

            def full_columns(index):
                pieces = [
                    windows(index, q, slab)[:, owner * window + skips[q] : (owner + 1) * window]
                    for owner in range(owners)
                    for q in range(4)
                ]
                return jnp.concatenate(pieces, axis=1)

            out_gate, out_up = full_columns(1), full_columns(2)
        return (
            mixed,
            grad_tokens,
            out_query,
            out_key,
            out_value,
            out_out,
            out_gate,
            out_up,
            out_down,
            *vectors,
        )

    return body


def solution(mesh):
    ctx, fsdp = mesh.shape["ctx"], mesh.shape["fsdp"]
    sizes = {"cz": ctx // (2 * CORES), "cy": 2, "core": CORES, "outer": fsdp // 2, "pair": 2}
    fine = Mesh(mesh.devices.reshape(tuple(sizes.values())), tuple(sizes))
    ctx_axes = ("cz", "cy", "core")
    fsdp_axes = ("outer", "pair")
    in_specs = (
        P(fsdp_axes, ctx_axes, None),
        P(fsdp_axes, ctx_axes),
        P(fsdp_axes, ctx_axes, None),
        *[P(fsdp_axes, None)] * 7,
        *[P(fsdp_axes)] * 5,
    )
    out_specs = (
        P(fsdp_axes, ctx_axes, None),
        P(fsdp_axes, ctx_axes, None),
        *[P(fsdp_axes, None)] * 7,
        *[P(fsdp_axes)] * 5,
    )
    return jax.shard_map(
        make_body(sizes), mesh=fine, in_specs=in_specs, out_specs=out_specs, check_vma=False
    )
```

```python
import functools

import jax
import jax.numpy as jnp
from jax import lax
from jax.experimental import pallas as pl
from jax.experimental.pallas import tpu as pltpu
from jax.sharding import Mesh, PartitionSpec as P

Q_HEADS = 14
KV_HEADS = 2
HEAD_DIM = 64
GROUP = Q_HEADS // KV_HEADS
HALF = HEAD_DIM // 2
BLK = 32
CORES = 2
Q_WIDTH = GROUP * HEAD_DIM

epsilon = 1e-06
theta = 1000000.0
scale = HEAD_DIM ** (-0.5)

BF = jnp.bfloat16
F32 = jnp.float32
CHIPS = ("cz", "cy")
VMEM = 56 * 1024 * 1024
SWAP = [(0, 1), (1, 0)]
NT = (((1,), (1,)), ((), ()))
TN = (((0,), (0,)), ((), ()))


def swap(values, axis):
    return lax.ppermute(values, axis, SWAP)


def dot(left, right, dims=(((1,), (0,)), ((), ()))):
    return lax.dot_general(left, right, dims, preferred_element_type=F32)


def rms_scale(rows, gain):
    inverse = lax.rsqrt(jnp.mean(rows * rows, axis=-1, keepdims=True) + epsilon)
    return rows * inverse * gain


def project_kernel(
    own_ref, far_ref, gain_ref, w_ref, b_ref, cos_ref, sin_ref, first_ref, q_ref, kv_ref
):
    own = pl.program_id(0) < pl.num_programs(0) // 2
    rows = jnp.where(own, own_ref[...].astype(F32), far_ref[...].astype(F32))
    first = rms_scale(rows, gain_ref[...]).astype(BF)
    first_ref[...] = first
    pre = dot(first, w_ref[...]) + b_ref[...]
    turned = Q_WIDTH + HEAD_DIM
    cosine = jnp.concatenate([cos_ref[...]] * (turned // 128), axis=1)
    sine = jnp.concatenate([sin_ref[...]] * (turned // 128), axis=1)
    front = pre[:, :turned]
    lane = lax.broadcasted_iota(jnp.int32, front.shape, 1) % HEAD_DIM
    other = jnp.where(
        lane < HALF, pltpu.roll(front, turned - HALF, 1), pltpu.roll(front, HALF, 1)
    )
    rot = front * cosine + other * sine
    q_ref[...] = (rot[:, :Q_WIDTH] * scale).astype(BF)
    kv_ref[...] = jnp.concatenate([rot[:, Q_WIDTH:], pre[:, turned:]], axis=1).astype(BF)


def project(own, far, gain, weight, bias, cosine, sine):
    count, width = 2 * own.shape[0], own.shape[1]
    wide = weight.shape[1]
    step = 256
    last = own.shape[0] // step - 1
    row_block = lambda n: pl.BlockSpec((step, n), lambda i: (i, 0))
    whole = lambda a, b: pl.BlockSpec((a, b), lambda i: (0, 0))
    return pl.pallas_call(
        project_kernel,
        grid=(count // step,),
        in_specs=[
            pl.BlockSpec((step, width), lambda i: (jnp.minimum(i, last), 0)),
            pl.BlockSpec((step, width), lambda i: (jnp.maximum(i - last - 1, 0), 0)),
            whole(1, width),
            whole(width, wide),
            whole(1, wide),
            row_block(128),
            row_block(128),
        ],
        out_specs=[row_block(width), row_block(Q_WIDTH), row_block(2 * HEAD_DIM)],
        out_shape=[
            jax.ShapeDtypeStruct((count, width), BF),
            jax.ShapeDtypeStruct((count, Q_WIDTH), BF),
            jax.ShapeDtypeStruct((count, 2 * HEAD_DIM), BF),
        ],
        compiler_params=pltpu.CompilerParams(vmem_limit_bytes=VMEM),
        cost_estimate=pl.CostEstimate(
            flops=2 * count * width * wide, bytes_accessed=count * width * 4, transcendentals=0
        ),
    )(own, far, gain, weight, bias, cosine, sine)


def stack_heads(flat):
    return jnp.concatenate(
        [flat[:, h * HEAD_DIM : (h + 1) * HEAD_DIM] for h in range(GROUP)], axis=0
    )


def run_order(starts_ref, seq, index):
    one, two = starts_ref[seq, 2 * index], starts_ref[seq, 2 * index + 1]
    late = jnp.where(one > two, BLK, 0)
    low = pl.multiple_of(late, BLK)
    high = pl.multiple_of(BLK - late, BLK)
    return low, high, jnp.minimum(one, two), jnp.maximum(one, two)


def load_rows(own_ref, seq, ref):
    lows, highs = [], []
    for i in range(2):
        low, high, _, _ = run_order(own_ref, seq, i)
        lows.append(ref[i, 0, pl.ds(low, BLK), :])
        highs.append(ref[i, 0, pl.ds(high, BLK), :])
    return [stack_heads(jnp.concatenate(rows, axis=0)) for rows in (lows, highs)]


def store_rows(own_ref, seq, ref, lows, highs):
    for i in range(2):
        low, high, _, _ = run_order(own_ref, seq, i)
        ref[i, 0, pl.ds(low, BLK), :] = lows[i * BLK : (i + 1) * BLK].astype(BF)
        ref[i, 0, pl.ds(high, BLK), :] = highs[i * BLK : (i + 1) * BLK].astype(BF)


def load_keys(starts_ref, own_ref, seq, kv_ref, keys_ref, low_ref, high_ref):
    half = keys_ref.shape[0] // 2
    wide = low_ref.shape[1]
    lane = lax.broadcasted_iota(jnp.int32, (1, wide), 1) % (2 * BLK)
    inside = lax.broadcasted_iota(jnp.int32, (BLK, wide), 0)
    _, _, low_a, high_a = run_order(own_ref, seq, 0)
    _, _, low_b, high_b = run_order(own_ref, seq, 1)
    low_pos = jnp.where(lane < BLK, low_a, low_b) + lane % BLK
    high_pos = jnp.where(lane < BLK, high_a, high_b) + lane % BLK
    for r in range(half // BLK):
        low, high, low_start, high_start = run_order(starts_ref, seq, r)
        at = r * BLK
        keys_ref[at : at + BLK, :] = kv_ref[r // 2, r % 2, 0, pl.ds(low, BLK), :]
        keys_ref[half + at : half + at + BLK, :] = kv_ref[r // 2, r % 2, 0, pl.ds(high, BLK), :]
        low_ref[at : at + BLK, :] = jnp.where(inside + low_start <= low_pos, 0.0, -1e30)
        high_ref[at : at + BLK, :] = jnp.where(inside + high_start <= high_pos, 0.0, -1e30)


def query_chunks():
    total = GROUP * 2 * BLK
    return [(lo, min(lo + 256, total)) for lo in range(0, total, 256)]


def head_slices(values):
    return [values[:, at : at + 2 * BLK] for at in range(0, values.shape[1], 2 * BLK)]


def attend_kernel(
    offset, starts_ref, own_ref, q_ref, kv_ref, o_ref, lse_ref, keys_ref, low_ref, high_ref
):
    seq = pl.program_id(0) + offset
    half = keys_ref.shape[0] // 2
    load_keys(starts_ref, own_ref, seq, kv_ref, keys_ref, low_ref, high_ref)
    kv = keys_ref[...]
    key_low, key_high = kv[:half, :HEAD_DIM], kv[half:, :HEAD_DIM]
    value_t = kv.astype(F32).T[HEAD_DIM:].astype(BF)
    value_low, value_high = value_t[:, :half], value_t[:, half:]
    query_low, query_high = load_rows(own_ref, seq, q_ref)
    lows, highs = [], []
    for lo, hi in query_chunks():
        scores = dot(key_low, query_low[lo:hi], NT) + low_ref[:, : hi - lo]
        top = jnp.max(scores, axis=0, keepdims=True)
        expo = jnp.exp(scores - top)
        total = jnp.sum(expo, axis=0, keepdims=True)
        out = dot(value_low, expo.astype(BF)) / total
        lse_ref[0, 0:1, lo:hi] = top + jnp.log(total)
        lows += [part.T for part in head_slices(out)]
        first = dot(key_low, query_high[lo:hi], NT)
        second = dot(key_high, query_high[lo:hi], NT) + high_ref[:, : hi - lo]
        top = jnp.maximum(
            jnp.max(first, axis=0, keepdims=True), jnp.max(second, axis=0, keepdims=True)
        )
        first, second = jnp.exp(first - top), jnp.exp(second - top)
        total = jnp.sum(first, axis=0, keepdims=True) + jnp.sum(second, axis=0, keepdims=True)
        out = (dot(value_low, first.astype(BF)) + dot(value_high, second.astype(BF))) / total
        lse_ref[0, 1:2, lo:hi] = top + jnp.log(total)
        highs += [part.T for part in head_slices(out)]
    store_rows(
        own_ref, seq, o_ref, jnp.concatenate(lows, axis=1), jnp.concatenate(highs, axis=1)
    )


def attend_back_kernel(
    offset,
    starts_ref,
    own_ref,
    q_ref,
    kv_ref,
    do_ref,
    lse_ref,
    cos_ref,
    sin_ref,
    dq_ref,
    dkv_ref,
    keys_ref,
    low_ref,
    high_ref,
    probs_ref,
    grads_ref,
):
    seq = pl.program_id(0) + offset
    half = keys_ref.shape[0] // 2
    wide = probs_ref.shape[1] // 2
    total = GROUP * 2 * BLK
    load_keys(starts_ref, own_ref, seq, kv_ref, keys_ref, low_ref, high_ref)
    kv = keys_ref[...]
    key_low, key_high = kv[:half, :HEAD_DIM], kv[half:, :HEAD_DIM]
    value_low, value_high = kv[:half, HEAD_DIM:], kv[half:, HEAD_DIM:]
    key_t = kv.astype(F32).T[:HEAD_DIM].astype(BF)
    query_low, query_high = load_rows(own_ref, seq, q_ref)
    out_low, out_high = load_rows(own_ref, seq, do_ref)

    def tables(ref):
        table = ref[0]
        lows, highs = [], []
        for i in range(2):
            one, two = own_ref[seq, 2 * i], own_ref[seq, 2 * i + 1]
            front = table[:, 2 * i * BLK : (2 * i + 1) * BLK]
            back = table[:, (2 * i + 1) * BLK : (2 * i + 2) * BLK]
            lows.append(jnp.where(one > two, back, front))
            highs.append(jnp.where(one > two, front, back))
        return jnp.concatenate(lows, axis=1), jnp.concatenate(highs, axis=1)

    cos_low, cos_high = tables(cos_ref)
    sin_low, sin_high = tables(sin_ref)

    def unturned(grad_q, cosine, sine):
        heads = []
        for part in head_slices(grad_q):
            front, back = part[:HALF], part[HALF:]
            heads.append(
                jnp.concatenate(
                    [front * cosine + back * sine, back * cosine - front * sine], axis=0
                ).T
            )
        return heads

    lows, highs = [], []
    for lo, hi in query_chunks():
        scores = dot(key_low, query_low[lo:hi], NT) + low_ref[:, : hi - lo]
        probs = jnp.exp(scores - lse_ref[0, 0:1, lo:hi])
        probs_ref[:half, lo:hi] = probs.astype(BF)
        grad_p = dot(value_low, out_low[lo:hi], NT)
        inner = jnp.sum(probs * grad_p, axis=0, keepdims=True)
        grad_s = (probs * (grad_p - inner)).astype(BF)
        grads_ref[:half, lo:hi] = grad_s
        lows += unturned(dot(key_t[:, :half], grad_s) * scale, cos_low, sin_low)
        lse = lse_ref[0, 1:2, lo:hi]
        at, to = wide + lo, wide + hi
        first = jnp.exp(dot(key_low, query_high[lo:hi], NT) - lse)
        second = jnp.exp(dot(key_high, query_high[lo:hi], NT) + high_ref[:, : hi - lo] - lse)
        probs_ref[:half, at:to] = first.astype(BF)
        probs_ref[half:, at:to] = second.astype(BF)
        grad_first = dot(value_low, out_high[lo:hi], NT)
        grad_second = dot(value_high, out_high[lo:hi], NT)
        inner = jnp.sum(first * grad_first, axis=0, keepdims=True) + jnp.sum(
            second * grad_second, axis=0, keepdims=True
        )
        grad_first = (first * (grad_first - inner)).astype(BF)
        grad_second = (second * (grad_second - inner)).astype(BF)
        grads_ref[:half, at:to] = grad_first
        grads_ref[half:, at:to] = grad_second
        grad_q = dot(key_t[:, :half], grad_first) + dot(key_t[:, half:], grad_second)
        highs += unturned(grad_q * scale, cos_high, sin_high)
    store_rows(
        own_ref, seq, dq_ref, jnp.concatenate(lows, axis=1), jnp.concatenate(highs, axis=1)
    )

    def key_grads(ref, left, right):
        low = dot(ref[:half, :total], left) + dot(ref[:half, wide : wide + total], right)
        return low, dot(ref[half:, wide : wide + total], right)

    key_parts = key_grads(grads_ref, query_low, query_high)
    value_parts = key_grads(probs_ref, out_low, out_high)
    grad_low, grad_high = [
        jnp.concatenate([key, value], axis=1).astype(BF)
        for key, value in zip(key_parts, value_parts)
    ]
    for r in range(half // BLK):
        low, high, _, _ = run_order(starts_ref, seq, r)
        at = r * BLK
        dkv_ref[r // 2, r % 2, 0, pl.ds(low, BLK), :] = grad_low[at : at + BLK]
        dkv_ref[r // 2, r % 2, 0, pl.ds(high, BLK), :] = grad_high[at : at + BLK]


def attention(back, offset, seqs, starts, own, q, kv, *more):
    run = q.shape[2]
    assert run == 2 * BLK
    chips = kv.shape[0]
    local = 2 * run
    keys = chips * local
    total = GROUP * local
    wide = 512
    q_spec = pl.BlockSpec((2, 1, run, Q_WIDTH), lambda s, st, ow: (0, s + offset, 0, 0))
    part_spec = pl.BlockSpec((2, 1, run, Q_WIDTH), lambda s, st, ow: (0, s, 0, 0))
    kv_block = (chips, 2, 1, run, 2 * HEAD_DIM)
    kv_spec = pl.BlockSpec(kv_block, lambda s, st, ow: (0, 0, s + offset, 0, 0))
    kv_part_spec = pl.BlockSpec(kv_block, lambda s, st, ow: (0, 0, s, 0, 0))
    lse_spec = pl.BlockSpec((1, 2, wide), lambda s, st, ow: (s + offset, 0, 0))
    turn_spec = pl.BlockSpec((1, HALF, local), lambda s, st, ow: (s + offset, 0, 0))
    in_specs = [q_spec, kv_spec]
    scratch = [
        pltpu.VMEM((keys, 2 * HEAD_DIM), BF),
        pltpu.VMEM((keys // 2, 256), F32),
        pltpu.VMEM((keys // 2, 256), F32),
    ]
    part_shape = jax.ShapeDtypeStruct((2, seqs, run, Q_WIDTH), BF)
    if back:
        in_specs += [q_spec, lse_spec, turn_spec, turn_spec]
        out_specs = [part_spec, kv_part_spec]
        kv_shape = kv.shape[:2] + (seqs,) + kv.shape[3:]
        out_shape = [part_shape, jax.ShapeDtypeStruct(kv_shape, BF)]
        scratch += [pltpu.VMEM((keys, 2 * wide), BF)] * 2
    else:
        out_specs = [part_spec, lse_spec]
        out_shape = [part_shape, jax.ShapeDtypeStruct((seqs, 2, wide), F32)]
    passes = 5 if back else 2
    return pl.pallas_call(
        functools.partial(attend_back_kernel if back else attend_kernel, offset),
        grid_spec=pltpu.PrefetchScalarGridSpec(
            num_scalar_prefetch=2,
            grid=(seqs,),
            in_specs=in_specs,
            out_specs=out_specs,
            scratch_shapes=scratch,
        ),
        out_shape=out_shape,
        compiler_params=pltpu.CompilerParams(vmem_limit_bytes=VMEM),
        cost_estimate=pl.CostEstimate(
            flops=8 * passes * seqs * keys * total * HEAD_DIM,
            bytes_accessed=seqs * keys * 512,
            transcendentals=seqs * keys * total,
        ),
    )(starts, own, q, kv, *more)


def mlp_kernel(s_ref, c_ref, g_ref, u_ref, d_ref, hid_ref, gg_ref, gu_ref, mix_ref, gs_ref):
    rows = s_ref[...]
    grad = c_ref[...]
    wide = g_ref.shape[1]
    for lo in range(0, wide, 256):
        hi = min(lo + 256, wide)
        gate = dot(rows, g_ref[:, lo:hi])
        up = dot(rows, u_ref[:, lo:hi])
        grad_hidden = dot(grad, d_ref[lo:hi, :], NT)
        sig = 1.0 / (1.0 + jnp.exp(-gate))
        silu = gate * sig
        hid_ref[:, lo:hi] = (silu * up).astype(BF)
        gg_ref[:, lo:hi] = (grad_hidden * up * (sig * (1.0 + gate * (1.0 - sig)))).astype(BF)
        gu_ref[:, lo:hi] = (grad_hidden * silu).astype(BF)
    mix_ref[...] = dot(hid_ref[...], d_ref[...]).astype(BF)
    gs_ref[...] = (dot(gg_ref[...], g_ref[...], NT) + dot(gu_ref[...], u_ref[...], NT)).astype(BF)


def mlp(rows, grad, gate_w, up_w, down_w):
    count, width = rows.shape
    wide = gate_w.shape[1]
    step = 256
    row_block = lambda n: pl.BlockSpec((step, n), lambda i: (i, 0))
    whole = lambda a, b: pl.BlockSpec((a, b), lambda i: (0, 0))
    shape = lambda n: jax.ShapeDtypeStruct((count, n), BF)
    return pl.pallas_call(
        mlp_kernel,
        grid=(count // step,),
        in_specs=[
            row_block(width),
            row_block(width),
            whole(width, wide),
            whole(width, wide),
            whole(wide, width),
        ],
        out_specs=[row_block(wide)] * 3 + [row_block(width)] * 2,
        out_shape=[shape(wide)] * 3 + [shape(width)] * 2,
        compiler_params=pltpu.CompilerParams(vmem_limit_bytes=VMEM),
        cost_estimate=pl.CostEstimate(
            flops=12 * count * width * wide,
            bytes_accessed=count * (wide * 6 + width * 8),
            transcendentals=count * wide,
        ),
    )(rows, grad, gate_w, up_w, down_w)


def weight_grad_kernel(pair_ref, a_near, a_far, b_near, b_far, keep_ref, send_ref, acc_ref):
    step = pl.program_id(0)
    steps = pl.num_programs(0)

    @pl.when(step == 0)
    def _():
        acc_ref[...] = dot(a_near[...], b_near[...], TN)

    @pl.when(jnp.logical_and(step > 0, step < steps // 2))
    def _():
        acc_ref[...] += dot(a_near[...], b_near[...], TN)

    @pl.when(step >= steps // 2)
    def _():
        acc_ref[...] += dot(a_far[...], b_far[...], TN)

    @pl.when(step == steps - 1)
    def _():
        outer, parts, tall, _ = keep_ref.shape
        tiles = acc_ref.shape[1] // 128
        high = tall // tiles
        slab = parts * high
        for out_ref, which in ((keep_ref, pair_ref[0]), (send_ref, 1 - pair_ref[0])):
            for o in range(outer):
                start = pl.multiple_of((2 * o + which) * slab, slab)
                for t in range(tiles):
                    tile = acc_ref[pl.ds(start, slab), t * 128 : (t + 1) * 128].astype(BF)
                    for z in range(parts):
                        out_ref[o, z, t * high : (t + 1) * high, :] = tile[
                            z * high : (z + 1) * high
                        ]


def weight_grad(pair, outer, parts, near, far):
    (a_near, b_near), (a_far, b_far) = near, far
    count, high = a_near.shape
    wide = b_near.shape[1]
    half = 2
    step = count // half
    tall = high // (2 * outer * parts) * (wide // 128)
    near_block = lambda n: pl.BlockSpec((step, n), lambda i, p: (jnp.minimum(i, half - 1), 0))
    far_block = lambda n: pl.BlockSpec((step, n), lambda i, p: (jnp.maximum(i - half, 0), 0))
    out_spec = pl.BlockSpec((outer, parts, tall, 128), lambda i, p: (0, 0, 0, 0))
    shape = jax.ShapeDtypeStruct((outer, parts, tall, 128), BF)
    return pl.pallas_call(
        weight_grad_kernel,
        grid_spec=pltpu.PrefetchScalarGridSpec(
            num_scalar_prefetch=1,
            grid=(2 * half,),
            in_specs=[near_block(high), far_block(high), near_block(wide), far_block(wide)],
            out_specs=[out_spec, out_spec],
            scratch_shapes=[pltpu.VMEM((high, wide), F32)],
        ),
        out_shape=[shape, shape],
        compiler_params=pltpu.CompilerParams(vmem_limit_bytes=VMEM),
        cost_estimate=pl.CostEstimate(
            flops=4 * count * high * wide,
            bytes_accessed=4 * count * (high + wide),
            transcendentals=0,
        ),
    )(pair, a_near, a_far, b_near, b_far)


def spread_rows_kernel(skip, in_ref, out_ref):
    parts, windows, _, tall, _ = in_ref.shape
    tiles = out_ref.shape[1] // 128
    high = tall // tiles
    for q in range(windows):
        drop = skip if q == windows - 1 else 0
        for z in range(parts):
            lo = max(drop - z * high, 0)
            if lo >= high:
                continue
            at = q * parts * high + z * high + lo - drop
            for t in range(tiles):
                out_ref[at : at + high - lo, t * 128 : (t + 1) * 128] = in_ref[
                    z, q, 0, t * high + lo : (t + 1) * high, :
                ].astype(F32)


def spread_rows(every, skip, part):
    parts, windows, _, tall, _ = every.shape
    width = tall * parts * 128 // ((part + skip) // windows)
    return pl.pallas_call(
        functools.partial(spread_rows_kernel, skip),
        grid=(1,),
        in_specs=[pl.BlockSpec((parts, windows, 1, tall, 128), lambda i: (0, 0, 0, 0, 0))],
        out_specs=pl.BlockSpec((part, width), lambda i: (0, 0)),
        out_shape=jax.ShapeDtypeStruct((part, width), F32),
        compiler_params=pltpu.CompilerParams(vmem_limit_bytes=VMEM),
    )(every)


def spread_columns_kernel(owners, part, begins, skips, gate_ref, up_ref, gate_out, up_out):
    high = gate_out.shape[0]
    tiles = gate_ref.shape[3] // high // owners
    for in_ref, out_ref in ((gate_ref, gate_out), (up_ref, up_out)):
        for owner in range(owners):
            for q in range(4):
                for t in range(skips[q] // 128, tiles):
                    at = owner * part + begins[q] + 128 * t
                    row = (owner * tiles + t) * high
                    out_ref[:, at : at + 128] = in_ref[0, q, 0, row : row + high, :].astype(F32)


def spread_columns(every, owners, part, begins, skips):
    parts, _, _, tall, _ = every.shape
    window = part - begins[3]
    high = tall * 128 // (owners * window)
    block = (1, 4, 1, tall, 128)
    out_spec = pl.BlockSpec((high, owners * part), lambda z: (z, 0))
    shape = jax.ShapeDtypeStruct((parts * high, owners * part), F32)
    return pl.pallas_call(
        functools.partial(spread_columns_kernel, owners, part, begins, skips),
        grid=(parts,),
        in_specs=[
            pl.BlockSpec(block, lambda z: (z, 0, 1, 0, 0)),
            pl.BlockSpec(block, lambda z: (z, 0, 2, 0, 0)),
        ],
        out_specs=[out_spec, out_spec],
        out_shape=[shape, shape],
        compiler_params=pltpu.CompilerParams(vmem_limit_bytes=VMEM),
    )(every, every)


def gather_small(values, axis, size):
    out = values[None]
    index = lax.axis_index(axis)
    bit = 1
    while bit < size:
        other = lax.ppermute(out, axis, [(i, i ^ bit) for i in range(size)])
        low = (index & bit) == 0
        out = jnp.where(
            low, jnp.concatenate([out, other], axis=0), jnp.concatenate([other, out], axis=0)
        )
        bit *= 2
    return out


def line_part(values, at):
    at = jnp.clip(at, 0, values.shape[0] - 1)
    return lax.dynamic_index_in_dim(values, at, 0, keepdims=False).astype(F32)


def line_load(values, axis, step, arrived):
    size = values.shape[0]
    index = lax.axis_index(axis)
    far = size - 1 - step
    up, down = line_part(values, index + far), line_part(values, index - far)
    if step:
        up, down = up + arrived[0].astype(F32), down + arrived[1].astype(F32)
    return up.astype(BF), down.astype(BF)


def line_send(load, axis, size, step):
    far = size - 1 - step
    right = [(i, i + 1) for i in range(size - 1) if i <= step]
    left = [(i + 1, i) for i in range(size - 1) if i + 1 >= far]
    return lax.ppermute(load[0], axis, right), lax.ppermute(load[1], axis, left)


def line_total(values, axis, arrived):
    own = line_part(values, lax.axis_index(axis))
    return (own + arrived[0].astype(F32) + arrived[1].astype(F32)).astype(BF)


def line_gather(values, axis, size):
    index = lax.axis_index(axis)
    right = left = values
    rights, lefts = [], []
    for step in range(size - 1):
        right = lax.ppermute(right, axis, [(i, i + 1) for i in range(size - 1) if i >= step])
        left = lax.ppermute(
            left, axis, [(i + 1, i) for i in range(size - 1) if i + 1 <= size - 1 - step]
        )
        rights.append(right)
        lefts.append(left)
    row = jnp.stack(rights[::-1] + [values] + lefts)
    return lax.dynamic_slice_in_dim(row, size - 1 - index, size, 0)


def pair_sum(values, axis, size):
    bit = 1
    while bit < size:
        other = lax.ppermute(values, axis, [(i, i ^ bit) for i in range(size)])
        values = (values.astype(F32) + other.astype(F32)).astype(values.dtype)
        bit *= 2
    return values


def together(*values):
    return lax.optimization_barrier(values)


def make_body(sizes):
    cz, outer = sizes["cz"], sizes["outer"]
    chips = cz * sizes["cy"]
    owners = 2 * outer

    def ordered(axis, own, other):
        low = lax.axis_index(axis) == 0
        return jnp.where(low, own, other), jnp.where(low, other, own)

    def gather_rows(values):
        rows = values.shape[0]
        if outer > 1:
            values = lax.all_gather(values, "outer", axis=0)
        else:
            values = values[None]
        both = jnp.stack(ordered("pair", values, swap(values, "pair")), axis=1)
        return both.reshape((owners * rows,) + values.shape[2:])

    def gather_start(values):
        if outer > 1:
            values = lax.all_gather(values, "outer", axis=0)
        else:
            values = values[None]
        return swap(values, "pair")

    def gather_finish(values, far):
        if outer > 1:
            values = lax.all_gather(values, "outer", axis=0)
        else:
            values = values[None]
        both = jnp.stack(ordered("pair", values, far), axis=1)
        return both.reshape((owners * values.shape[1],) + values.shape[2:])

    def gather_chips(values):
        return lax.all_gather(values, CHIPS, axis=0)

    def split_cy(values, axis):
        half = values.shape[axis] // 2
        first = lax.slice_in_dim(values, 0, half, axis=axis)
        last = lax.slice_in_dim(values, half, 2 * half, axis=axis)
        low = lax.axis_index("cy") == 0
        return jnp.where(low, first, last), jnp.where(low, last, first)

    def split_owners(values):
        split = values.reshape(outer, 2, -1, values.shape[1])
        if outer > 1:
            split = lax.psum_scatter(split, "outer", scatter_dimension=0)
        else:
            split = split[0]
        low = lax.axis_index("pair") == 0
        return jnp.where(low, split[0], split[1]), jnp.where(low, split[1], split[0])

    def add(left, right):
        return (left.astype(F32) + right.astype(F32)).astype(left.dtype)

    def bits_of(size):
        return [1 << b for b in range((size - 1).bit_length())]

    def exchange(values, axis, size, bit):
        return lax.ppermute(values, axis, [(i, i ^ bit) for i in range(size)])

    def body(
        tokens,
        positions,
        cotangent,
        query_weight,
        key_weight,
        value_weight,
        out_weight,
        gate_weight,
        up_weight,
        down_weight,
        query_bias,
        key_bias,
        value_bias,
        first_gain,
        second_gain,
    ):
        core0 = lax.axis_index("core") == 0
        pair = lax.axis_index("pair")
        quarter = 2 * lax.axis_index("cy") + lax.axis_index("core")
        seqs, run, width = tokens.shape
        rows = seqs * run
        ff = gate_weight.shape[1]
        part = down_weight.shape[0]
        window = min(part, -(-part // 512) * 128)
        begins = [min(q * window, part - window) for q in range(4)]
        skips = [min(q * window - begins[q], window) for q in range(4)]
        slab = gate_weight.shape[0]

        def heads_of(values, each):
            return jnp.where(core0, values[..., :each], values[..., each:])

        places = jnp.stack([positions, swap(positions, "core")])
        firsts = places[:, :, ::BLK]
        starts = gather_small(gather_small(firsts, "cy", 2), "cz", cz)
        starts = starts.transpose(3, 0, 1, 2, 4).reshape(seqs, -1)
        own_starts = firsts.transpose(1, 0, 2).reshape(seqs, 4)
        turned = Q_WIDTH + HEAD_DIM
        kv_rows = key_bias.shape[0]
        vectors = jnp.concatenate([query_bias, key_bias, value_bias, first_gain, second_gain])
        lanes = vectors.shape[0]
        wide = turned + HEAD_DIM
        lines = -(-lanes // wide)
        vectors = jnp.concatenate([vectors, jnp.zeros((16 * wide - lanes,), BF)]).reshape(16, wide)
        qkv_local = jnp.concatenate(
            [
                jnp.concatenate(
                    [
                        heads_of(query_weight, Q_WIDTH),
                        heads_of(key_weight, HEAD_DIM),
                        heads_of(value_weight, HEAD_DIM),
                    ],
                    axis=1,
                ),
                vectors,
            ]
        )
        tokens_far = swap(tokens, "core")
        def by_quarter(choices):
            out = choices[3]
            for q in range(3):
                out = jnp.where(quarter == q, choices[q], out)
            return out

        def columns(values, q):
            at = [owner * part + begins[q] for owner in range(owners)]
            return jnp.concatenate([values[:, a : a + window] for a in at], axis=1)

        inside = lax.broadcasted_iota(jnp.int32, (1, owners * window), 1) % window
        skip = by_quarter([jnp.int32(n) for n in skips])

        def units(values):
            full = by_quarter([columns(values, q) for q in range(4)])
            return jnp.where(inside < skip, jnp.zeros((), BF), full)

        gate_own = units(gate_weight)
        up_own = units(up_weight)
        down_own = by_quarter([down_weight[at : at + window] for at in begins])
        qkv_all = gather_rows(qkv_local)
        qkv_all, gate_own, up_own, out_own, down_own, starts, own_starts = lax.optimization_barrier(
            (qkv_all, gate_own, up_own, out_weight, down_own, starts, own_starts)
        )
        qkv_all = qkv_all.reshape(owners, slab + 16, wide)
        qkv = qkv_all[:, :slab].reshape(owners * slab, wide)
        vectors = qkv_all[:, slab:].reshape(owners, -1)

        def vector_of(at, size):
            return vectors[:, at : at + size].reshape(-1)

        qb = vector_of(0, slab)
        kb = vector_of(slab, kv_rows)
        vb = vector_of(slab + kv_rows, kv_rows)
        fgain = vector_of(slab + 2 * kv_rows, slab).astype(F32)
        sgain = vector_of(2 * slab + 2 * kv_rows, slab).astype(F32)
        bias = jnp.concatenate(
            [heads_of(qb, Q_WIDTH), heads_of(kb, HEAD_DIM), heads_of(vb, HEAD_DIM)]
        ).astype(F32)[None]
        if outer > 1:
            out_full = gather_rows(out_own)
            out_w = jnp.where(core0, out_full[:Q_WIDTH], out_full[Q_WIDTH:])
        else:
            out_far = lax.ppermute(out_own, ("core", "pair"), [(0, 1), (3, 2)])
            out_w = jnp.where(lax.axis_index("core") == pair, out_own, out_far)
        down_w = gather_rows(down_own)

        freq = theta ** (-jnp.arange(HALF, dtype=F32) / HALF)
        angles = places.reshape(2 * rows, 1).astype(F32) * freq
        cosine, sine = jnp.cos(angles), jnp.sin(angles)
        cos_wide = jnp.concatenate([cosine] * 4, axis=1)
        sin_wide = jnp.concatenate([-sine, sine] * 2, axis=1)

        def turned_rows(table):
            table = table.reshape(2, seqs, run, HALF).transpose(1, 3, 0, 2)
            return table.reshape(seqs, HALF, 2 * run)

        own_rows = tokens.reshape(rows, width)
        first, q, kv = project(
            own_rows, tokens_far.reshape(rows, width), fgain[None], qkv, bias, cos_wide, sin_wide
        )
        q = q.reshape(2, seqs, run, Q_WIDTH)
        kv = kv.reshape(2, seqs, run, 2 * HEAD_DIM)
        cut = seqs // 2
        kv_all = gather_chips(kv)
        gate_far = gather_start(gate_own)
        kv_all, out_w, down_w, gate_far, cot_late, up_own = together(
            kv_all, out_w, down_w, gate_far, cotangent, up_own
        )
        up_far = gather_start(up_own)
        grad_own = cot_late.reshape(rows, width)
        far_grad = swap(grad_own, "cy")
        attn, lse = attention(False, 0, seqs, starts, own_starts, q, kv_all)
        attn_rows = attn.reshape(2 * rows, Q_WIDTH)
        attn_rows, up_far, far_grad = together(attn_rows, up_far, far_grad)
        gate_w = gather_finish(gate_own, gate_far)
        up_w = gather_finish(up_own, up_far)
        attn_part = dot(attn_rows, out_w).astype(BF)
        inputs = own_rows.astype(F32)
        middle = (
            inputs
            + attn_part[:rows].astype(F32)
            + swap(attn_part[rows:], "core").astype(F32)
        )

        second = rms_scale(middle, sgain).astype(BF)
        near_c = jnp.concatenate([grad_own, swap(grad_own, "core")])
        far_c = jnp.concatenate([far_grad, swap(far_grad, "core")])
        far_second = swap(second, "cy")
        near_s = jnp.concatenate([second, swap(second, "core")])
        near_h, near_g, near_u, near_mix, near_gs = mlp(near_s, near_c, gate_w, up_w, down_w)
        far_second, near_h, near_g, near_u, near_mix, near_gs = together(
            far_second, near_h, near_g, near_u, near_mix, near_gs
        )
        far_core, gs_core = together(swap(far_second, "core"), swap(near_gs[rows:], "core"))
        far_s = jnp.concatenate([far_second, far_core])
        far_h, far_g, far_u, far_mix, far_gs = mlp(far_s, far_c, gate_w, up_w, down_w)
        own_gs = near_gs[:rows].astype(F32) + gs_core.astype(F32)
        send_gs = add(far_gs[:rows], swap(far_gs[rows:], "core"))

        send_gs, far_h, far_g, far_u, far_mix = together(send_gs, far_h, far_g, far_u, far_mix)
        back_gs = swap(send_gs, "cy")
        pair_index = jnp.reshape(pair, (1,)).astype(jnp.int32)

        def unit_grad(near, far):
            keep, send = weight_grad(pair_index, outer, cz, near, far)
            if outer > 1:
                keep = lax.psum_scatter(keep, "outer", scatter_dimension=0)
                send = lax.psum_scatter(send, "outer", scatter_dimension=0)
                return keep, send
            return keep[0], send[0]

        keep_down, send_down = unit_grad((near_h, near_c), (far_h, far_c))
        keep_down, send_down, far_g, near_mix, far_mix = together(
            keep_down, send_down, far_g, near_mix, far_mix
        )
        sum_down = swap(send_down, "pair")
        mix_near_core = swap(near_mix[rows:], "core")
        mix_far_core = swap(far_mix[rows:], "core")
        keep_gate, send_gate = unit_grad((near_s, near_g), (far_s, far_g))
        keep_gate, far_u = together(keep_gate, far_u)
        keep_up, send_up = unit_grad((near_s, near_u), (far_s, far_u))
        keep_up, back_gs, sum_down, mix_near_core, mix_far_core, send_gate, send_up = together(
            keep_up, back_gs, sum_down, mix_near_core, mix_far_core, send_gate, send_up
        )
        sum_gate, sum_up = swap(send_gate, "pair"), swap(send_up, "pair")
        send_mix = add(far_mix[:rows], mix_far_core)
        back_mix = swap(send_mix, "cy")
        grad_second = own_gs + back_gs.astype(F32)
        _, pull_second = jax.vjp(rms_scale, middle, sgain)
        grad_middle_part, grad_sgain = pull_second(grad_second)
        grad_middle = grad_own.astype(F32) + grad_middle_part
        grad_branch = grad_middle.astype(BF)
        grad_branch = jnp.concatenate([grad_branch, swap(grad_branch, "core")])
        grad_attn = dot(grad_branch, out_w, NT).astype(BF).reshape(2, seqs, run, Q_WIDTH)
        grad_out_w = dot(attn_rows, grad_branch, TN).astype(BF)
        cos_t, sin_t = turned_rows(cosine), turned_rows(sine)

        def attend_back(at, count, grad):
            return attention(True, at, count, starts, own_starts, q, kv_all, grad, lse, cos_t, sin_t)

        def keys_cy(values):
            return split_cy(values.reshape((cz, 2) + values.shape[1:]), 1)

        grad_q_near, grad_kv_near = attend_back(0, cut, grad_attn)
        grad_q_near, grad_kv_near, back_mix, sum_down, sum_gate, sum_up = together(
            grad_q_near, grad_kv_near, back_mix, sum_down, sum_gate, sum_up
        )
        mix_own = near_mix[:rows].astype(F32) + mix_near_core.astype(F32)
        mixed = (middle + mix_own + back_mix.astype(F32)).astype(BF).reshape(seqs, run, width)
        line = jnp.concatenate(
            [add(keep_down, sum_down), add(keep_gate, sum_gate), add(keep_up, sum_up)], axis=1
        )
        if outer > 1:
            every_out = jnp.concatenate(ordered("core", grad_out_w, swap(grad_out_w, "core")))
            keep_out, send_out = split_owners(every_out)
            out_rows = add(keep_out, swap(send_out, "pair"))
        else:
            far_out = lax.ppermute(grad_out_w, ("core", "pair"), [(1, 0), (2, 3)])
            out_rows = add(grad_out_w, far_out)
            mine_here = lax.axis_index("core") == pair
            out_rows = jnp.where(mine_here, out_rows, swap(out_rows, "core"))
        out_rows = heads_of(out_rows, width // 2)

        keep_near, send_near = keys_cy(grad_kv_near)
        load = line_load(line, "cz", 0, None)
        keep_out, send_out = split_cy(out_rows, 0)
        load, send_near, grad_late, send_out = together(load, send_near, grad_attn, send_out)
        far_out = swap(send_out, "cy")
        arrived = line_send(load, "cz", cz, 0)
        back_near = swap(send_near, "cy")
        grad_q_far, grad_kv_far = attend_back(cut, seqs - cut, grad_late)
        grad_q_far, grad_kv_far, arrived, back_near, far_out = together(
            grad_q_far, grad_kv_far, arrived, back_near, far_out
        )
        out_sum = add(keep_out, far_out)
        grad_q = jnp.concatenate([grad_q_near, grad_q_far], axis=1).reshape(2 * rows, Q_WIDTH)
        grad_q_w = dot(first, grad_q, TN).astype(BF)
        keep_far, send_far = keys_cy(grad_kv_far)
        keep_early, send_early = split_owners(grad_q_w)
        bits = bits_of(cz)
        load = line_load(line, "cz", 1, arrived)
        load, send_far, out_sum = together(load, send_far, out_sum)
        arrived, back_far, far_out = together(
            line_send(load, "cz", cz, 1),
            swap(send_far, "cy"),
            exchange(out_sum, "cz", cz, bits[0]),
        )
        out_sum = add(out_sum, far_out)
        keys = [add(keep_near, back_near), add(keep_far, back_far)]
        keys = jnp.concatenate(keys, axis=3).reshape(cz, 2 * rows, 2 * HEAD_DIM)
        load, keys_load = line_load(line, "cz", 2, arrived), line_load(keys, "cz", 0, None)
        load, keys_load, send_early, out_sum = together(load, keys_load, send_early, out_sum)
        arrived, keys_arrived, far_early, far_out = together(
            line_send(load, "cz", cz, 2),
            line_send(keys_load, "cz", cz, 0),
            swap(send_early, "pair"),
            exchange(out_sum, "cz", cz, bits[1]),
        )
        out_sum = add(out_sum, far_out)
        for bit in bits[2:]:
            out_sum = add(out_sum, exchange(out_sum, "cz", cz, bit))
        for step in range(3, cz - 1):
            arrived = line_send(line_load(line, "cz", step, arrived), "cz", cz, step)
        mine = line_total(line, "cz", arrived)
        early = add(keep_early, far_early)
        keep_early, send_early = split_cy(early, 0)
        keys_load = line_load(keys, "cz", 1, keys_arrived)
        mine, keys_load, send_early, out_sum = together(mine, keys_load, send_early, out_sum)
        keys_arrived, far_early, far_out = together(
            line_send(keys_load, "cz", cz, 1), swap(send_early, "cy"), swap(out_sum, "cy")
        )
        out_sum = jnp.concatenate(ordered("cy", out_sum, far_out))
        early = add(keep_early, far_early)
        for step in range(2, cz - 1):
            load = line_load(keys, "cz", step, keys_arrived)
            if step == 2:
                load, early, out_sum = together(load, early, out_sum)
                keys_arrived, far_early, far_sum = together(
                    line_send(load, "cz", cz, step),
                    exchange(early, "cz", cz, bits[0]),
                    swap(out_sum, "core"),
                )
                early = add(early, far_early)
            else:
                keys_arrived = line_send(load, "cz", cz, step)
        grad_kv = line_total(keys, "cz", keys_arrived).astype(F32)
        front = grad_kv[:, :HALF]
        back = grad_kv[:, HALF:HEAD_DIM]
        grad_kv = jnp.concatenate(
            [front * cosine + back * sine, back * cosine - front * sine, grad_kv[:, HEAD_DIM:]],
            axis=1,
        ).astype(BF)
        grad_qkv = jnp.concatenate([grad_q, grad_kv], axis=1)
        grad_kv_w = dot(first, grad_kv, TN).astype(BF)
        grad_biases = jnp.sum(grad_qkv.astype(F32), axis=0)
        grad_first_part = dot(grad_qkv, qkv, NT).astype(BF)
        keep_kv, send_kv = split_owners(grad_kv_w)
        for bit in bits[2:]:
            early = add(early, exchange(early, "cz", cz, bit))
        send_first, send_kv = together(grad_first_part[rows:], send_kv)
        far_early = exchange(early, "cz", cz, bits[1])
        far_first, far_kv = together(swap(send_first, "core"), swap(send_kv, "pair"))
        total_kv = add(keep_kv, far_kv)
        grad_first = grad_first_part[:rows].astype(F32) + far_first.astype(F32)
        _, pull_first = jax.vjp(rms_scale, inputs, fgain)
        grad_input_part, grad_fgain = pull_first(grad_first)
        grad_tokens = (grad_middle + grad_input_part).reshape(seqs, run, width)

        zeros = jnp.zeros((), F32)

        def spread(values):
            return jnp.concatenate(
                [jnp.where(core0, values, zeros), jnp.where(core0, zeros, values)]
            )

        vector = jnp.concatenate(
            [
                spread(grad_biases[:Q_WIDTH]),
                spread(grad_biases[Q_WIDTH:turned]),
                spread(grad_biases[turned:]),
                grad_fgain,
                grad_sgain,
            ]
        )
        hops = [("cz", cz, bit) for bit in bits] + [("cy", 2, 1)]
        for count, hop in enumerate(hops):
            total_kv, vector = together(total_kv, vector)
            last = count == len(hops) - 1
            sends = [exchange(total_kv, *hop), exchange(vector, *hop)] + [far_early] * last
            arrivals = together(*sends)
            total_kv, vector = add(total_kv, arrivals[0]), vector + arrivals[1]
            if last:
                early = add(early, arrivals[2])
        total_kv, vector = together(total_kv, vector)
        far_kv, far_vector, far_early = together(
            swap(total_kv, "core"), swap(vector, "core"), swap(early, "cy")
        )
        early = jnp.concatenate(ordered("cy", early, far_early))
        far_early = swap(early, "core")
        vector = vector + far_vector
        vector = pair_sum(vector, "pair", 2)
        if outer > 1:
            vector = pair_sum(vector, "outer", outer)
        out_query = jnp.concatenate(
            ordered("core", early.astype(F32), far_early.astype(F32)), axis=1
        )
        out_out = jnp.concatenate(
            ordered("core", out_sum.astype(F32), far_sum.astype(F32)), axis=1
        )
        low_kv, high_kv = ordered("core", total_kv.astype(F32), far_kv.astype(F32))
        out_key = jnp.concatenate([low_kv[:, :HEAD_DIM], high_kv[:, :HEAD_DIM]], axis=1)
        out_value = jnp.concatenate([low_kv[:, HEAD_DIM:], high_kv[:, HEAD_DIM:]], axis=1)
        owner = 2 * lax.axis_index("outer") + pair
        vectors = []
        at = 0
        for size in (width, KV_HEADS * HEAD_DIM, KV_HEADS * HEAD_DIM, width, width):
            share = size // owners
            vectors.append(lax.dynamic_slice(vector, (at + owner * share,), (share,)))
            at += size

        every = lax.all_gather(mine, CHIPS + ("core",), axis=0)
        every = every.reshape((cz, 4, 3, -1, 128))
        if part % 128 == 0 and not any(skips[:3]):
            out_down = spread_rows(every, skips[3], part)
            out_gate, out_up = spread_columns(every, owners, part, begins, skips)
        else:

            def windows(index, q, high):
                tiles = every[:, q, index].reshape(cz, -1, high // cz, 128)
                return tiles.transpose(0, 2, 1, 3).reshape(high, -1).astype(F32)

            out_down = jnp.concatenate(
                [windows(0, q, window)[skips[q] :] for q in range(4)]
            )

            def full_columns(index):
                pieces = [
                    windows(index, q, slab)[:, owner * window + skips[q] : (owner + 1) * window]
                    for owner in range(owners)
                    for q in range(4)
                ]
                return jnp.concatenate(pieces, axis=1)

            out_gate, out_up = full_columns(1), full_columns(2)
        return (
            mixed,
            grad_tokens,
            out_query,
            out_key,
            out_value,
            out_out,
            out_gate,
            out_up,
            out_down,
            *vectors,
        )

    return body


def solution(mesh):
    ctx, fsdp = mesh.shape["ctx"], mesh.shape["fsdp"]
    sizes = {"cz": ctx // (2 * CORES), "cy": 2, "core": CORES, "outer": fsdp // 2, "pair": 2}
    fine = Mesh(mesh.devices.reshape(tuple(sizes.values())), tuple(sizes))
    ctx_axes = ("cz", "cy", "core")
    fsdp_axes = ("outer", "pair")
    in_specs = (
        P(fsdp_axes, ctx_axes, None),
        P(fsdp_axes, ctx_axes),
        P(fsdp_axes, ctx_axes, None),
        *[P(fsdp_axes, None)] * 7,
        *[P(fsdp_axes)] * 5,
    )
    out_specs = (
        P(fsdp_axes, ctx_axes, None),
        P(fsdp_axes, ctx_axes, None),
        *[P(fsdp_axes, None)] * 7,
        *[P(fsdp_axes)] * 5,
    )
    return jax.shard_map(
        make_body(sizes), mesh=fine, in_specs=in_specs, out_specs=out_specs, check_vma=False
    )
```
